128 devices in a mesh: tp: 4 (over y_hi, core), ep: 32 (over x, y_lo, z).
Axes of the slice: x: 4, y: 4 (y_hi: 2, y_lo: 2; y = y_hi * 2 + y_lo), z: 4, core: 2. Of those that a mesh axis runs over, the one named last changes fastest.
Arguments:
- tokens: bfloat16 [1024, 7168], P(('ep', 'tp')), may hold values from -6 to 6
- routes: int32 [1024, 2], P(('ep', 'tp')), may hold values from 0 to 3, all different within a row; in each aligned block of 8 rows (0 to 7, 8 to 15, ...) at most 8 rows name the same one
- gate_weights: float32 [1024, 2], P(('ep', 'tp')), may hold values from 0.1 to 1
- dense_gate: bfloat16 [7168, 2560], P('ep', 'tp'), may hold values from -0.0625 to 0.0625
- dense_up: bfloat16 [7168, 2560], P('ep', 'tp'), may hold values from -0.0625 to 0.0625
- dense_down: bfloat16 [7168, 2560], P('ep', 'tp'), may hold values from -0.125 to 0.125
- expert_gate: bfloat16 [4, 4864, 7168], P('tp', 'ep'), may hold values from -0.0625 to 0.0625
- expert_up: bfloat16 [4, 4864, 7168], P('tp', 'ep'), may hold values from -0.0625 to 0.0625
- expert_down: bfloat16 [4, 4864, 7168], P('tp', 'ep'), may hold values from -0.078125 to 0.078125
Outputs:
- mixed: bfloat16 [1024, 7168], P(('ep', 'tp'))
The draws below stay inside these ranges and needn't reach their ends.
Inputs may be any that keep to these rules, and one draw needn't show every extreme that they name: `routes`: the 2 experts of a token differ. Among the 8 tokens of one device (aligned blocks of rows) no expert is named more than 8 times, and in every draw some expert is named exactly 8 times in some block; every expert is named by some token.
All inputs are finite; a program needn't handle non-finite values.
Results may differ from the reference program's by a relative error of at most 0.02.
Values may be sent and summed in bfloat16 or wider, within the bound.
A program may use at most 192 MiB of HBM per device.

```python
import math
import jax
import jax.numpy as jnp
import numpy as np
from jax import lax

D = 7168
FFD = 2560
EXP_FF = 4864
TOP = 2
TOK_DEV = 8
EXPERTS = 4
CAP = 8
TOKENS = 1024
N_TP = 4
N_EP = 32


def block_levels(key, extent, cuts, least, top_value):
    def one(position, shards_of):
        steps = jax.random.uniform(jax.random.fold_in(jax.random.fold_in(key, 6), position), (shards_of,), jnp.float32, least / len(cuts), top_value / len(cuts))
        return jnp.repeat(jnp.exp(steps), extent[position] // shards_of).reshape((-1,) + (1,) * (len(extent) - position - 1))

    level = one(*cuts[0])
    for cut in cuts[1:]:
        level = level * one(*cut)
    return level


def routed_block(own_key, own, number, rows, number_of, top, reach, skew):
    ranking = jax.random.permutation(own_key, number_of)
    crowded, usual = shares(number_of, rows * top, reach, skew, True), shares(number_of, rows * top, reach, skew, False)
    places = jnp.arange(number_of)

    def named(lengths, turn):
        used = int((lengths > 0).sum())
        fixed = max(1, used // 4)
        passed = fixed + (places - fixed + turn * (used - fixed)) % max(1, number_of - fixed)
        return jnp.zeros((number_of,), jnp.int32).at[ranking[jnp.where(places < fixed, places, passed)]].set(jnp.asarray(lengths, jnp.int32))

    lengths = jnp.where(number % 4 == 0, named(crowded, number // 4), named(usual, number - number // 4 - 1))
    mixed = jax.random.permutation(jax.random.fold_in(own, 3), number_of)
    source_of, sink = mixed[0:number_of // 2 * 2:2], mixed[1:number_of // 2 * 2:2]
    margin = jnp.minimum(lengths[source_of] - 1, reach - lengths[sink]) // 2
    margin = jnp.where((source_of == ranking[0]) | (sink == ranking[0]) | (lengths[sink] == 0), 0, jnp.maximum(margin, 0))
    passed = jax.random.randint(jax.random.fold_in(own, 4), (number_of // 2,), 0, 1 << 20) % (margin + 1)
    lengths = lengths.at[source_of].add(-passed).at[sink].add(passed)
    items = jnp.searchsorted(jnp.cumsum(lengths), jnp.arange(rows * top), side="right").astype(jnp.int32)
    table = items.reshape(top, rows).T
    table = table[jax.random.permutation(jax.random.fold_in(own, 1), rows)]
    turn = jax.random.randint(jax.random.fold_in(own, 2), (rows, 1), 0, top)
    return jnp.take_along_axis(table, (jnp.arange(top)[None, :] + turn) % top, axis=1)


def shares(number_of, total, reach, skew, full):
    weights = [(1 << 20) // math.isqrt(standing ** skew) + 1 for standing in range(1, number_of + 1)]
    largest = reach if full else min(reach, max(-(-total // number_of), total * weights[0] // sum(weights)))
    least = 1 if total - largest >= number_of - 1 else 0
    counts, spare = [largest] + [least] * (number_of - 1), total - largest - least * (number_of - 1)
    while spare > 0:
        free = [i for i in range(1, number_of) if counts[i] < largest] or [i for i in range(1, number_of) if counts[i] < reach]
        mass, remaining = sum([weights[i] for i in free]), spare
        for i in free:
            addition = min(reach - counts[i], max(1, remaining * weights[i] // mass), spare)
            counts[i] = counts[i] + addition
            spare = spare - addition
    return np.array(counts)


def noise(own_key, dims, scale, limit, shards=(), dtype=jnp.bfloat16):
    values = scale * jax.random.normal(own_key, dims, jnp.float32)
    if shards:
        values = values * block_levels(own_key, dims, shards, -0.22, 0.18)
    return jnp.clip(values, -limit, limit).astype(dtype)


def setup_inputs(seed: int = 0) -> dict:
    arg_keys = jax.random.split(jax.random.key(seed), 10)
    tokens = noise(arg_keys[0], (TOKENS, D), 1.0, 6.0, ((0, 128),))
    routes_keys = jax.random.split(jax.random.fold_in(arg_keys[1], 1), TOKENS // TOK_DEV)
    routes_turns = jax.random.permutation(jax.random.fold_in(arg_keys[1], 3), TOKENS // TOK_DEV)
    routes = jax.vmap(lambda own, number: routed_block(jax.random.fold_in(arg_keys[1], 2), own, number, TOK_DEV, EXPERTS, TOP, CAP, 2))(routes_keys, routes_turns).reshape((TOKENS, TOP))
    gate_weights = jnp.clip(jnp.exp(math.log(1.0) - 2.3025851 * jax.random.uniform(arg_keys[2], (TOKENS, TOP), jnp.float32) ** block_levels(arg_keys[2], (TOKENS, TOP), ((0, 128),), -0.2, 0.2)), 0.1, 1.0)
    dense_gate = noise(arg_keys[3], (D, FFD), D ** -0.5, 0.0625, ((0, 32), (1, 4)))
    dense_up = noise(arg_keys[4], (D, FFD), D ** -0.5, 0.0625, ((0, 32), (1, 4)))
    dense_down = noise(arg_keys[5], (D, FFD), FFD ** -0.5, 0.125, ((0, 32), (1, 4)))
    expert_gate = noise(arg_keys[6], (EXPERTS, EXP_FF, D), D ** -0.5, 0.0625, ((0, 4), (1, 32)))
    expert_up = noise(arg_keys[7], (EXPERTS, EXP_FF, D), D ** -0.5, 0.0625, ((0, 4), (1, 32)))
    expert_down = noise(arg_keys[8], (EXPERTS, EXP_FF, D), EXP_FF ** -0.5, 0.078125, ((0, 4), (1, 32)))
    return dict(tokens=tokens, routes=routes, gate_weights=gate_weights, dense_gate=dense_gate, dense_up=dense_up, dense_down=dense_down, expert_gate=expert_gate, expert_up=expert_up, expert_down=expert_down)


def reference(tokens, routes, gate_weights, dense_gate, dense_up, dense_down, expert_gate, expert_up, expert_down):
    gate_vals = jnp.dot(tokens, dense_gate, preferred_element_type=jnp.float32)
    up_vals = jnp.dot(tokens, dense_up, preferred_element_type=jnp.float32)
    dense_hidden = (jax.nn.silu(gate_vals) * up_vals).astype(jnp.bfloat16)
    group_width = FFD // N_TP
    dense_out = jnp.zeros(tokens.shape, jnp.float32)
    for tp_index in range(N_TP):
        lower = tp_index * group_width
        partial_value = jnp.dot(dense_hidden[:, lower:lower + group_width], dense_down[:, lower:lower + group_width].T, preferred_element_type=jnp.float32)
        dense_out = dense_out + partial_value.astype(jnp.bfloat16).astype(jnp.float32)
    slab_width = EXP_FF // N_EP
    routed = jnp.zeros(tokens.shape, jnp.float32)
    for expert in range(EXPERTS):
        chosen = (routes == expert).astype(jnp.float32)
        factor = jnp.sum(chosen * gate_weights.astype(jnp.float32), axis=1)
        e_gate = jnp.dot(tokens, expert_gate[expert].T, preferred_element_type=jnp.float32)
        e_up = jnp.dot(tokens, expert_up[expert].T, preferred_element_type=jnp.float32)
        e_hidden = (jax.nn.silu(e_gate) * e_up).astype(jnp.bfloat16)
        hidden_groups = jnp.transpose(e_hidden.reshape(tokens.shape[0], N_EP, slab_width), (1, 0, 2))
        down_groups = expert_down[expert].reshape(N_EP, slab_width, tokens.shape[1])

        def add_group(total, pieces):
            hidden_piece, down_piece = pieces
            term = jnp.dot(hidden_piece, down_piece, preferred_element_type=jnp.float32)
            return total + term.astype(jnp.bfloat16).astype(jnp.float32), None

        summed, _ = lax.scan(add_group, jnp.zeros(tokens.shape, jnp.float32), (hidden_groups, down_groups))
        expert_out = summed.astype(jnp.bfloat16).astype(jnp.float32)
        routed = routed + factor[:, None] * expert_out
    return (tokens.astype(jnp.float32) + dense_out + routed).astype(jnp.bfloat16)
```

```python
import jax
import jax.numpy as jnp
from jax import lax
from jax.experimental import pallas as pl
from jax.experimental.pallas import tpu as pltpu
from jax.sharding import PartitionSpec as P

MESH = pl.DeviceIdType.MESH
BF = jnp.bfloat16
F32 = jnp.float32

WIDTH = 7168
HALF = WIDTH // 2
ROWS = 16
UNITS = 192
DENSE_ROWS = 32
EXPERT_ROWS = 152
OUT_COLS = (1280, 1152, 1152)
OFFSET = (0, 1280, 2432)
IN_COLS = (1280, 1152, 1280)
CUT = 640
ORDER = (("y", "x", "z"), ("z", "y", "x"), ("x", "z", "y"))
PARTS = range(3)


def kernel(
    tokens,
    routes,
    weights,
    dense,
    expert_gate,
    expert_up,
    expert_down,
    out,
    x0, x1, x2,
    o0, o1, o2,
    r0, r1, r2,
    *rest,
):
    xs, os, rs = (x0, x1, x2), (o0, o1, o2), (r0, r1, r2)
    rel = [[rest[k * 12 + p * 4:k * 12 + p * 4 + 4] for p in PARTS] for k in range(3)]
    rest = rest[36:]
    (raw, wg, wu, wd, ga, ua, hid, tok_out, tok_in, fin_out, fin_in,
     w_sem, ag_s, ag_r, sib_s, sib_r, rs_s, rs_r, sum_s, sum_r, end_s, end_r) = rest

    ep, tp = lax.axis_index("ep"), lax.axis_index("tp")
    core = lax.rem(tp, 2)
    other = 1 - core
    pos = {
        "x": lax.div(ep, 8),
        "y": lax.div(tp, 2) * 2 + lax.rem(lax.div(ep, 4), 2),
        "z": lax.rem(ep, 4),
    }

    def device(x, y, z, c):
        return {"ep": x * 8 + lax.rem(y, 2) * 4 + z, "tp": lax.div(y, 2) * 2 + c}

    def moved(axis, by):
        place = dict(pos)
        place[axis] = lax.rem(pos[axis] + by, 4)
        return device(place["x"], place["y"], place["z"], core)

    right = {a: moved(a, 1) for a in "xyz"}
    left = {a: moved(a, 3) for a in "xyz"}
    sibling = {"ep": ep, "tp": lax.div(tp, 2) * 2 + other}

    raws = [expert_gate, expert_up, expert_down]
    loads = []
    for n, w in enumerate((wg, wu, wd)):
        loads.append(pltpu.make_async_copy(raws[n].at[0], raw.at[n], w_sem.at[n]))
        for h in range(2):
            loads.append(pltpu.make_async_copy(
                dense.at[n, :, pl.ds(h * HALF, HALF)], w.at[h, pl.ds(0, DENSE_ROWS)], w_sem.at[3 + 2 * n + h]))
    for load in loads:
        load.start()

    barrier = pltpu.get_barrier_semaphore()
    for a in "xyz":
        pl.semaphore_signal(barrier, inc=1, device_id=right[a], device_id_type=MESH)
        pl.semaphore_signal(barrier, inc=1, device_id=left[a], device_id_type=MESH)
    pl.semaphore_signal(barrier, inc=1, device_id=sibling, device_id_type=MESH)
    pl.semaphore_wait(barrier, 7)

    pending = []

    def send(src, dst, s_sem, r_sem, to):
        copy = pltpu.make_async_remote_copy(
            src_ref=src, dst_ref=dst, send_sem=s_sem, recv_sem=r_sem, device_id=to, device_id_type=MESH)
        copy.start()
        pending.append(copy)
        return copy

    lane = lax.broadcasted_iota(jnp.int32, (8, 128), 1)
    named = lax.div(lane, 2)
    factor = jnp.where(routes[:, 0:1] == named, weights[:, 0:1], 0.0) + jnp.where(
        routes[:, 1:2] == named, weights[:, 1:2], 0.0)
    high = factor.astype(BF).astype(F32)
    factor = jnp.where(lax.rem(lane, 2) == 0, high, factor - high)
    tok_out[:, pl.ds(0, HALF)] = tokens[:, pl.ds(pl.multiple_of(other * HALF, 128), HALF)].astype(F32)
    tok_out[:, pl.ds(HALF, 128)] = factor
    swap = send(tok_out, tok_in, end_s.at[0], end_r.at[0], sibling)
    coords = [[pos[a] for a in ORDER[p]] for p in PARTS]
    swap.wait_recv()
    for p in PARTS:
        i1, i2, i3 = coords[p]
        mine = tokens[:, pl.ds(pl.multiple_of(core * HALF + OFFSET[p], 128), OUT_COLS[p])].astype(F32)
        if IN_COLS[p] > OUT_COLS[p]:
            mine = jnp.concatenate([mine, factor], axis=1)
        theirs = tok_in[:, pl.ds(OFFSET[p], IN_COLS[p])]
        first = jnp.where(core == 0, mine, theirs)
        second = jnp.where(core == 0, theirs, mine)
        xs[p][core, i3, i2, i1] = jnp.concatenate([first, second], axis=0).astype(BF)

    def block(p, k, value):
        i1, i2, i3 = coords[p]
        if k == 0:
            return xs[p].at[core, i3, i2, value]
        if k == 1:
            return xs[p].at[core, i3, value]
        return xs[p].at[core, value]

    def half(ref, k, part, cols):
        if k == 0:
            return ref.at[:, pl.ds(0, CUT)] if part == 0 else ref.at[:, pl.ds(CUT, cols - CUT)]
        return ref.at[pl.ds(2 * part, 2)]

    def ring(p, k):
        axis = ORDER[p][k]
        me = pos[axis]
        return axis, me, lax.rem(me + 1, 4), lax.rem(me + 3, 4), lax.rem(me + 2, 4)

    A, B = 0, 1
    flights = {}

    def launch(p, k):
        axis, me, _, _, _ = ring(p, k)
        own = block(p, k, me)
        for part, to, slot in ((A, right, 0), (B, left, 3), (B, right, 1), (A, left, 2)):
            piece = half(own, k, part, IN_COLS[p])
            flights[p, k, slot] = send(piece, piece, ag_s.at[p, k, slot], ag_r.at[p, k, slot], to[axis])

    def relay(p, k):
        axis, me, plus, minus, _ = ring(p, k)
        flights[p, k, 0].wait_recv()
        piece = half(block(p, k, minus), k, A, IN_COLS[p])
        flights[p, k, 4] = send(piece, piece, ag_s.at[p, k, 4], ag_r.at[p, k, 4], right[axis])
        flights[p, k, 3].wait_recv()
        piece = half(block(p, k, plus), k, B, IN_COLS[p])
        flights[p, k, 5] = send(piece, piece, ag_s.at[p, k, 5], ag_r.at[p, k, 5], left[axis])

    shares = {}

    def share(p, n, ref):
        shares[p, n] = send(ref, ref, sib_s.at[p, n], sib_r.at[p, n], sibling)

    def gate_up(p, value, h):
        cols = OUT_COLS[p]
        rows = xs[p][h, value, :, :, :, pl.ds(0, cols)].reshape(256, cols)
        for w, acc in ((wg, ga), (wu, ua)):
            piece = lax.dot_general(
                rows, w[h, :, pl.ds(OFFSET[p], cols)], (((1,), (1,)), ((), ())), preferred_element_type=F32)
            for i in range(4):
                for j in range(4):
                    at = where(p, value, i, j)
                    n = (i * 4 + j) * ROWS
                    acc[at] += piece[n:n + ROWS]

    def where(p, value, second, first):
        place = dict(zip(ORDER[p], (first, second, value)))
        return place["y"], place["z"], place["x"]

    for k in range(2):
        for p in PARTS:
            launch(p, k)
        if k == 1:
            for load in loads:
                load.wait()
            for n, w in enumerate((wg, wu, wd)):
                for h in range(2):
                    w[h, pl.ds(176, 16)] = jnp.zeros((16, HALF), BF)
                    w[h, pl.ds(DENSE_ROWS, EXPERT_ROWS)] = raw[n, :, pl.ds(h * HALF, HALF)]
            ga[...] = jnp.zeros_like(ga)
            ua[...] = jnp.zeros_like(ua)
        for p in PARTS:
            relay(p, k)
        for p in PARTS:
            for slot in (1, 2, 4, 5):
                flights[p, k, slot].wait_recv()

    k = 2
    for p in PARTS:
        launch(p, k)
        share(p, 0, block(p, k, ring(p, k)[1]))
    for p in PARTS:
        gate_up(p, ring(p, k)[1], core)
    for p in PARTS:
        relay(p, k)
        axis, me, plus, minus, _ = ring(p, k)
        share(p, 1, half(block(p, k, minus), k, A, IN_COLS[p]))
        share(p, 2, half(block(p, k, plus), k, B, IN_COLS[p]))
    for p in PARTS:
        shares[p, 0].wait_recv()
        gate_up(p, ring(p, k)[1], other)
    for p in PARTS:
        axis, me, plus, minus, _ = ring(p, k)
        flights[p, k, 1].wait_recv()
        share(p, 3, half(block(p, k, minus), k, B, IN_COLS[p]))
        flights[p, k, 2].wait_recv()
        share(p, 4, half(block(p, k, plus), k, A, IN_COLS[p]))
        gate_up(p, minus, core)
        gate_up(p, plus, core)
    for p in PARTS:
        axis, me, plus, minus, _ = ring(p, k)
        shares[p, 1].wait_recv()
        shares[p, 3].wait_recv()
        gate_up(p, minus, other)
        shares[p, 2].wait_recv()
        shares[p, 4].wait_recv()
        gate_up(p, plus, other)
    for p in PARTS:
        opposite = ring(p, k)[4]
        flights[p, k, 4].wait_recv()
        share(p, 5, half(block(p, k, opposite), k, A, IN_COLS[p]))
        flights[p, k, 5].wait_recv()
        share(p, 6, half(block(p, k, opposite), k, B, IN_COLS[p]))
        gate_up(p, opposite, core)
    for p in PARTS:
        shares[p, 5].wait_recv()
        shares[p, 6].wait_recv()
        gate_up(p, ring(p, k)[4], other)

    lanes = lax.broadcasted_iota(jnp.int32, (256, 128), 1)
    column = lax.broadcasted_iota(jnp.int32, (256, UNITS), 1)
    for y in range(4):
        sent = x2[0, y, :, :, :, pl.ds(OUT_COLS[2], 128)].reshape(256, 128).astype(F32)
        share_of = jnp.sum(jnp.where(lax.div(lanes, 2) == tp, sent, 0.0), axis=1, keepdims=True)
        g = ga[y].reshape(256, UNITS)
        u = ua[y].reshape(256, UNITS)
        value = g / (1.0 + jnp.exp(-g)) * u
        value = value * jnp.where(column < DENSE_ROWS, 1.0, share_of)
        hid[y] = value.astype(BF).reshape(4, 4, ROWS, UNITS)

    for copy in pending:
        copy.wait_send()
    pending.clear()

    def hidden_rows(p, value):
        return jnp.concatenate(
            [hid[where(p, value, i, j)] for i in range(4) for j in range(4)], axis=0)

    def chunks(p):
        return [(c, min(256, OUT_COLS[p] - c)) for c in range(0, OUT_COLS[p], 256)]

    swaps = {}

    def give(p, value, n):
        rows = hidden_rows(p, value)
        for c, size in chunks(p):
            piece = jnp.dot(rows, wd[other, :, pl.ds(OFFSET[p] + c, size)], preferred_element_type=F32)
            xs[p][0, value, :, :, :, pl.ds(c, size)] = piece.astype(BF).reshape(4, 4, ROWS, size)
        swaps[p, n] = send(
            xs[p].at[0, value, :, :, :, pl.ds(0, OUT_COLS[p])], rs[p].at[value], sum_s.at[p, n], sum_r.at[p, n], sibling)

    def keep(p, value, n):
        rows = hidden_rows(p, value)
        swaps[p, n].wait_recv()
        for c, size in chunks(p):
            piece = jnp.dot(rows, wd[core, :, pl.ds(OFFSET[p] + c, size)], preferred_element_type=F32)
            theirs = rs[p][value, :, :, :, pl.ds(c, size)].reshape(256, size).astype(F32)
            os[p][value, :, :, :, pl.ds(c, size)] = (piece + theirs).astype(BF).reshape(4, 4, ROWS, size)

    def add(ref, *more):
        total = ref[...].astype(F32)
        for one in more:
            total = total + one[...].astype(F32)
        ref[...] = total.astype(BF)

    def target(p, k, value):
        i1, i2, i3 = coords[p]
        if k == 2:
            return os[p].at[value]
        if k == 1:
            return os[p].at[i3, value]
        return os[p].at[i3, i2, value]

    sums = {}

    def toss(p, k, slot, src, dst, to):
        sums[p, k, slot] = send(src, dst, rs_s.at[p, k, slot], rs_r.at[p, k, slot], to)

    def first(p, k):
        axis, _, _, _, opposite = ring(p, k)
        rel_a, rel_b, _, _ = rel[k][p]
        cols = OUT_COLS[p]
        blk = target(p, k, opposite)
        toss(p, k, 0, half(blk, k, A, cols), rel_a, right[axis])
        toss(p, k, 1, half(blk, k, B, cols), rel_b, left[axis])

    def to_right_now(p, k):
        axis, _, plus, _, _ = ring(p, k)
        in_left = rel[k][p][2]
        cols = OUT_COLS[p]
        toss(p, k, 2, half(target(p, k, plus), k, B, cols), half(in_left, k, B, cols), right[axis])

    def to_left_now(p, k):
        axis, _, _, minus, _ = ring(p, k)
        in_right = rel[k][p][3]
        cols = OUT_COLS[p]
        toss(p, k, 3, half(target(p, k, minus), k, A, cols), half(in_right, k, A, cols), left[axis])

    def pass_on(p, k):
        axis, _, plus, minus, _ = ring(p, k)
        rel_a, rel_b, in_left, in_right = rel[k][p]
        cols = OUT_COLS[p]
        sums[p, k, 0].wait_recv()
        piece = half(target(p, k, plus), k, A, cols)
        add(piece, rel_a)
        toss(p, k, 4, piece, half(in_left, k, A, cols), right[axis])
        sums[p, k, 1].wait_recv()
        piece = half(target(p, k, minus), k, B, cols)
        add(piece, rel_b)
        toss(p, k, 5, piece, half(in_right, k, B, cols), left[axis])

    def arrived(p, k):
        for slot in (2, 3, 4, 5):
            sums[p, k, slot].wait_recv()

    k = 2
    order = [(p, n) for n in (4, 2, 3, 1) for p in PARTS]
    for step in range(len(order) + 1):
        if step < len(order):
            p, n = order[step]
            give(p, ring(p, k)[n], n)
        if step > 0:
            p, n = order[step - 1]
            keep(p, ring(p, k)[n], n)
            if n == 4:
                first(p, k)
            elif n == 2:
                to_right_now(p, k)
            elif n == 3:
                to_left_now(p, k)
                if p == 2:
                    for q in PARTS:
                        pass_on(q, k)
    for p in PARTS:
        arrived(p, k)
        add(target(p, k, ring(p, k)[1]), rel[k][p][2], rel[k][p][3])
        first(p, 1)
        to_right_now(p, 1)
        to_left_now(p, 1)
    for k in (1, 0):
        for p in PARTS:
            pass_on(p, k)
        for p in PARTS:
            arrived(p, k)
            if k == 1:
                add(target(p, k, ring(p, k)[1]), rel[k][p][2], rel[k][p][3])
                first(p, 0)
                to_right_now(p, 0)
                to_left_now(p, 0)
    here = []
    for p in PARTS:
        total = (target(p, 0, ring(p, 0)[1])[...].astype(F32) + rel[0][p][2][...].astype(F32)
                 + rel[0][p][3][...].astype(F32))
        low, high = total[0:8], total[8:16]
        here.append(jnp.where(core == 0, low, high))
        fin_out[:, pl.ds(OFFSET[p], OUT_COLS[p])] = jnp.where(core == 0, high, low)
    last = send(fin_out, fin_in, end_s.at[1], end_r.at[1], sibling)
    for p in PARTS:
        at = pl.ds(pl.multiple_of(core * HALF + OFFSET[p], 128), OUT_COLS[p])
        out[:, at] = (tokens[:, at].astype(F32) + here[p]).astype(BF)
    last.wait_recv()
    at = pl.ds(pl.multiple_of(other * HALF, 128), HALF)
    out[:, at] = (tokens[:, at].astype(F32) + fin_in[...]).astype(BF)
    for copy in pending:
        copy.wait_send()


def fused(tokens, routes, weights, dense, expert_gate, expert_up, expert_down):
    vmem = pl.BlockSpec(memory_space=pltpu.VMEM)
    hbm = pl.BlockSpec(memory_space=pl.ANY)
    cube = (4, 4, 4, ROWS)
    scratch = [pltpu.VMEM((2, *cube, IN_COLS[p]), BF) for p in PARTS]
    scratch += [pltpu.VMEM((*cube, OUT_COLS[p]), BF) for p in PARTS] * 2
    for k in range(3):
        for p in PARTS:
            cols = OUT_COLS[p]
            if k == 0:
                shapes = [(ROWS, CUT), (ROWS, cols - CUT), (ROWS, cols), (ROWS, cols)]
            elif k == 1:
                shapes = [(2, ROWS, cols)] * 2 + [(4, ROWS, cols)] * 2
            else:
                shapes = [(2, 4, ROWS, cols)] * 2 + [(4, 4, ROWS, cols)] * 2
            scratch += [pltpu.VMEM(s, BF) for s in shapes]
    scratch += [
        pltpu.VMEM((3, EXPERT_ROWS, WIDTH), BF),
        pltpu.VMEM((2, UNITS, HALF), BF),
        pltpu.VMEM((2, UNITS, HALF), BF),
        pltpu.VMEM((2, UNITS, HALF), BF),
        pltpu.VMEM((*cube, UNITS), F32),
        pltpu.VMEM((*cube, UNITS), F32),
        pltpu.VMEM((*cube, UNITS), BF),
        pltpu.VMEM((8, HALF + 128), F32),
        pltpu.VMEM((8, HALF + 128), F32),
        pltpu.VMEM((8, HALF), F32),
        pltpu.VMEM((8, HALF), F32),
        pltpu.SemaphoreType.DMA((9,)),
        pltpu.SemaphoreType.DMA((3, 3, 6)),
        pltpu.SemaphoreType.DMA((3, 3, 6)),
        pltpu.SemaphoreType.DMA((3, 7)),
        pltpu.SemaphoreType.DMA((3, 7)),
        pltpu.SemaphoreType.DMA((3, 3, 6)),
        pltpu.SemaphoreType.DMA((3, 3, 6)),
        pltpu.SemaphoreType.DMA((3, 5)),
        pltpu.SemaphoreType.DMA((3, 5)),
        pltpu.SemaphoreType.DMA((2,)),
        pltpu.SemaphoreType.DMA((2,)),
    ]
    return pl.pallas_call(
        kernel,
        out_shape=jax.ShapeDtypeStruct((8, WIDTH), BF),
        in_specs=[vmem, vmem, vmem, hbm, hbm, hbm, hbm],
        out_specs=vmem,
        scratch_shapes=scratch,
        cost_estimate=pl.CostEstimate(flops=2 * 1024 * 192 * 7168 * 3, bytes_accessed=8_000_000, transcendentals=1024 * 192),
        compiler_params=pltpu.CompilerParams(
            collective_id=0, has_side_effects=True, vmem_limit_bytes=63 * 2**20),
    )(tokens, routes, weights, dense, expert_gate, expert_up, expert_down)


def per_device(tokens, routes, gate_weights, dense_gate, dense_up, dense_down, expert_gate, expert_up, expert_down):
    n = lax.axis_size("ep")

    def own_units(weight):
        rows, units = weight.shape
        return weight.T.reshape(n, units // n, rows)

    packed = jnp.stack([own_units(w) for w in (dense_gate, dense_up, dense_down)], axis=1)
    there = lax.all_to_all(packed, "ep", split_axis=0, concat_axis=0, tiled=True)
    there = there.transpose(1, 2, 0, 3).reshape(3, packed.shape[2], tokens.shape[1])
    dense = jnp.pad(there, ((0, 0), (0, DENSE_ROWS - there.shape[1]), (0, 0)))
    return fused(tokens, routes, gate_weights, dense, expert_gate, expert_up, expert_down)


def solution(mesh):
    return jax.shard_map(
        per_device,
        mesh=mesh,
        in_specs=(
            P(("ep", "tp"), None),
            P(("ep", "tp"), None),
            P(("ep", "tp"), None),
            P("ep", "tp"),
            P("ep", "tp"),
            P("ep", "tp"),
            P("tp", "ep", None),
            P("tp", "ep", None),
            P("tp", "ep", None),
        ),
        out_specs=P(("ep", "tp"), None),
        check_vma=False,
    )
```

```python
import jax
import jax.numpy as jnp
from jax import lax
from jax.experimental import pallas as pl
from jax.experimental.pallas import tpu as pltpu
from jax.sharding import PartitionSpec as P

MESH = pl.DeviceIdType.MESH
BF = jnp.bfloat16
F32 = jnp.float32

WIDTH = 7168
HALF = WIDTH // 2
ROWS = 16
UNITS = 192
DENSE_ROWS = 32
EXPERT_ROWS = 152
DEPTH = 224
RUN = 4 * DEPTH
OUT_COLS = (1280, 1152, 1152)
OFFSET = (0, 1280, 2432)
IN_COLS = (1280, 1152, 1280)
CUT = 640
ORDER = (("y", "x", "z"), ("z", "y", "x"), ("x", "z", "y"))
PARTS = range(3)
OWN, RIGHT, LEFT, FAR = range(4)
BOTH = pl.ds(1, 2)
OTHERS = pl.ds(1, 3)
LINE = (0, OTHERS)
PLANE = ((0, 0), (0, OTHERS), (OTHERS, 0), (BOTH, OTHERS), (3, OTHERS))
A, B = 0, 1
FLIGHTS = 48


def cut(selected, part, cols):
    if part is None:
        return tuple(selected)
    if selected and selected[0] is BOTH:
        return (1 + part, *selected[1:])
    side = pl.ds(0, CUT) if part == A else pl.ds(CUT, cols - CUT)
    return (*selected, slice(None), side)


def view(ref, index):
    return ref.at[index] if index else ref


def kernel(
    tokens, routes, weights, packed, expert_gate, expert_up, expert_down,
    out,
    x0, x1, x2, o0, o1, o2, r0, r1, r2,
    *rest,
):
    xs, os, rs = (x0, x1, x2), (o0, o1, o2), (r0, r1, r2)
    passing = {(k, p): rest[(k - 1) * 3 + p] for k in (1, 2) for p in PARTS}
    sides = {(k, p): rest[6 + (k - 1) * 3 + p] for k in (1, 2) for p in PARTS}
    threes = {(k, p): rest[12 + k * 3 + p] for k in (0, 1) for p in PARTS}
    rest = rest[18:]
    (raw, wg, wu, wd, ga, ua, hid, tok_out, tok_in, fin_out, fin_in, dbuf,
     w_sem, d_s, d_r, out_s, ag_r, sib_r, rs_r, sum_r, end_r) = rest

    ep, tp = lax.axis_index("ep"), lax.axis_index("tp")
    core = lax.rem(tp, 2)
    other = 1 - core
    pos = {
        "x": lax.div(ep, 8),
        "y": lax.div(tp, 2) * 2 + lax.rem(lax.div(ep, 4), 2),
        "z": lax.rem(ep, 4),
    }

    def device(x, y, z):
        return {"ep": x * 8 + lax.rem(y, 2) * 4 + z, "tp": lax.div(y, 2) * 2 + core}

    def moved(axis, by):
        place = dict(pos)
        place[axis] = lax.rem(pos[axis] + by, 4)
        return device(place["x"], place["y"], place["z"])

    right = {a: moved(a, 1) for a in "xyz"}
    left = {a: moved(a, 3) for a in "xyz"}
    far = {a: moved(a, 2) for a in "xyz"}
    sibling = {"ep": ep, "tp": lax.div(tp, 2) * 2 + other}

    loads = [
        pltpu.make_async_copy(w.at[0], raw.at[n], w_sem.at[n])
        for n, w in enumerate((expert_gate, expert_up, expert_down))
    ]
    loads.append(pltpu.make_async_copy(packed.at[ep], dbuf.at[ep], d_r))
    for load in loads:
        load.start()

    y_low = lax.rem(pos["y"], 2)
    steps = sorted(
        ((dx, dy, dz) for dx in range(4) for dy in range(2) for dz in range(4) if dx or dy or dz),
        key=lambda d: min(d[0], 4 - d[0]) + d[1] + min(d[2], 4 - d[2]))

    def peer(dx, dy, dz):
        return lax.rem(pos["x"] + dx, 4) * 8 + lax.rem(y_low + dy, 2) * 4 + lax.rem(pos["z"] + dz, 4)

    peers = [peer(*d) for d in steps]

    barrier = pltpu.get_barrier_semaphore()
    pl.semaphore_signal(barrier, inc=1, device_id=sibling, device_id_type=MESH)
    for by in (1, 2, 3):
        pl.semaphore_signal(barrier, inc=1, device_id=moved("y", by), device_id_type=MESH)
    for d, to in zip(steps, peers):
        if d != (0, 1, 0):
            pl.semaphore_signal(barrier, inc=1, device_id={"ep": to, "tp": tp}, device_id_type=MESH)
    pl.semaphore_wait(barrier, 34)

    flying = []

    def send(src, dst, r_sem, to):
        n = len(flying)
        if n >= FLIGHTS:
            flying[n - FLIGHTS].wait_send()
        copy = pltpu.make_async_remote_copy(
            src_ref=src, dst_ref=dst, send_sem=out_s.at[n % FLIGHTS], recv_sem=r_sem, device_id=to, device_id_type=MESH)
        copy.start()
        flying.append(copy)
        return copy

    def settle():
        for copy in flying[max(0, len(flying) - FLIGHTS):]:
            copy.wait_send()
        flying.clear()

    def landed(ref, sem):
        pltpu.make_async_copy(ref, ref, sem).wait()

    diagonal = lax.broadcasted_iota(jnp.int32, (8, 8), 0) == lax.broadcasted_iota(jnp.int32, (8, 8), 1)

    def column_of(row):
        return jnp.sum(jnp.where(diagonal, jnp.broadcast_to(row, (8, 8)), jnp.zeros((8, 8), row.dtype)), axis=1, keepdims=True)

    lane = lax.broadcasted_iota(jnp.int32, (8, 128), 1)
    named = lax.div(lane, 2).astype(F32)
    chosen = [column_of(routes[n:n + 1, :].astype(F32)) for n in range(2)]
    factor = jnp.where(chosen[0] == named, column_of(weights[0:1, :]), 0.0) + jnp.where(
        chosen[1] == named, column_of(weights[1:2, :]), 0.0)
    high = factor.astype(BF).astype(F32)
    factor = jnp.where(lax.rem(lane, 2) == 0, high, factor - high)
    tok_out[:, pl.ds(0, HALF)] = tokens[:, pl.ds(pl.multiple_of(other * HALF, 128), HALF)].astype(F32)
    tok_out[:, pl.ds(HALF, 128)] = factor
    swap = send(tok_out, tok_in, end_r.at[0], sibling)
    swap.wait_recv()
    for p in PARTS:
        mine = tokens[:, pl.ds(pl.multiple_of(core * HALF + OFFSET[p], 128), OUT_COLS[p])].astype(F32)
        if IN_COLS[p] > OUT_COLS[p]:
            mine = jnp.concatenate([mine, factor], axis=1)
        theirs = tok_in[:, pl.ds(OFFSET[p], IN_COLS[p])]
        first = jnp.where(core == 0, mine, theirs)
        second = jnp.where(core == 0, theirs, mine)
        xs[p][core, 0, 0, 0] = jnp.concatenate([first, second], axis=0).astype(BF)

    def chunks_of(k):
        return ((),) if k == 0 else tuple((s,) for s in LINE) if k == 1 else PLANE

    def token_view(p, k, place, c, part=None):
        prefix = {0: (core, 0, 0, place), 1: (core, 0, place), 2: (core, place)}[k]
        return xs[p].at[(*prefix, *cut(chunks_of(k)[c], part, IN_COLS[p]))]

    def ag_slot(k, c, n):
        return 0 if k == 0 else (0, 1, 5)[k] + 2 * c + n

    def fly(p, k, c, n, src, dst, to):
        send(src, dst, ag_r.at[p, ag_slot(k, c, n)], to[ORDER[p][k]])

    def spread(p, k, c=0, direct=False):
        own = token_view(p, k, OWN, c)
        fly(p, k, c, 0, own, token_view(p, k, LEFT, c), right)
        fly(p, k, c, 0, own, token_view(p, k, RIGHT, c), left)
        if direct:
            fly(p, k, c, 1, own, token_view(p, k, FAR, c), far)

    def near(p, k, c=0):
        landed(token_view(p, k, OTHERS if k == 0 else BOTH, c), ag_r.at[p, ag_slot(k, c, 0)])

    def relay(p, k, c=0):
        near(p, k, c)
        fly(p, k, c, 1, token_view(p, k, LEFT, c, A), token_view(p, k, FAR, c, A), right)
        fly(p, k, c, 1, token_view(p, k, RIGHT, c, B), token_view(p, k, FAR, c, B), left)

    def distant(p, k, c=0):
        landed(token_view(p, k, FAR, c), ag_r.at[p, ag_slot(k, c, 1)])

    shares = {}

    def share(p, n, ref):
        shares[p, n] = send(ref, ref, sib_r.at[p, n], sibling)

    def where(p, third, second, first):
        place = dict(zip(ORDER[p], (first, second, third)))
        return place["y"], place["z"], place["x"]

    def gate_up(p, place, h):
        cols = OUT_COLS[p]
        rows = xs[p][h, place, :, :, :, pl.ds(0, cols)].reshape(256, cols)
        for w, acc in ((wg, ga), (wu, ua)):
            piece = lax.dot_general(
                rows, w[h, :, pl.ds(OFFSET[p], cols)], (((1,), (1,)), ((), ())), preferred_element_type=F32)
            for i in range(4):
                for j in range(4):
                    n = (i * 4 + j) * ROWS
                    acc[where(p, place, i, j)] += piece[n:n + ROWS]

    def dense_out(first, last):
        for to in peers[first:last]:
            pltpu.make_async_remote_copy(
                src_ref=packed.at[to], dst_ref=dbuf.at[ep], send_sem=d_s, recv_sem=d_r,
                device_id={"ep": to, "tp": tp}, device_id_type=MESH).start()

    def dense_in():
        landed(dbuf, d_r)
        row = lax.broadcasted_iota(jnp.int32, (ROWS, RUN), 0)
        for i in range(8):
            at = pl.ds((i % 4) * RUN, RUN)
            run = jnp.concatenate([dbuf[4 * i + z][:, 0:DEPTH].astype(F32) for z in range(4)], axis=1)
            tail = run[48:64]
            for n, w in enumerate((wg, wu, wd)):
                w[i // 4, pl.ds(0, 16), at] = run[16 * n:16 * n + 16].astype(BF)
                turned = tail if n == 0 else pltpu.roll(tail, 16 - 4 * n, 0)
                w[i // 4, pl.ds(16, 16), at] = jnp.where(row < 4, turned, 0.0).astype(BF)

    def expert_in():
        for load in loads[:3]:
            load.wait()
        for n, w in enumerate((wg, wu, wd)):
            for h in range(2):
                w[h, pl.ds(176, 16)] = jnp.zeros((16, HALF), BF)
                w[h, pl.ds(DENSE_ROWS, EXPERT_ROWS)] = raw[n, :, pl.ds(h * HALF, HALF)]
        ga[...] = jnp.zeros_like(ga)
        ua[...] = jnp.zeros_like(ua)

    for p in PARTS:
        spread(p, 0, direct=True)
    for p in PARTS:
        spread(p, 1, 0, direct=True)
    dense_out(0, 8)
    for p in PARTS:
        spread(p, 2, 0)
    dense_out(8, 16)
    for p in PARTS:
        near(p, 0)
        spread(p, 1, 1)
        spread(p, 2, 1)
    dense_out(16, 24)
    for p in PARTS:
        near(p, 1, 0)
        distant(p, 1, 0)
        spread(p, 2, 2)
    dense_out(24, 31)
    for p in PARTS:
        relay(p, 2, 0)
    for p in PARTS:
        relay(p, 1, 1)
        spread(p, 2, 3)
    for p in PARTS:
        distant(p, 1, 1)
        spread(p, 2, 4)
        share(p, 0, xs[p].at[core, 0])
    expert_in()
    for p in PARTS:
        relay(p, 2, 1)
    for p in PARTS:
        relay(p, 2, 2)
    dense_in()
    for p in PARTS:
        relay(p, 2, 3)
    for p in PARTS:
        gate_up(p, OWN, core)
    for p in PARTS:
        relay(p, 2, 4)
        share(p, 1, xs[p].at[core, RIGHT])
        share(p, 2, xs[p].at[core, LEFT])
    for p in PARTS:
        shares[p, 0].wait_recv()
        gate_up(p, OWN, other)
    for p in PARTS:
        gate_up(p, RIGHT, core)
        gate_up(p, LEFT, core)
    for p in PARTS:
        for c in (0, 1):
            distant(p, 2, c)
        share(p, 3, xs[p].at[core, FAR, 0])
    for p in PARTS:
        shares[p, 1].wait_recv()
        gate_up(p, RIGHT, other)
        shares[p, 2].wait_recv()
        gate_up(p, LEFT, other)
    for p in PARTS:
        for c in (2, 3, 4):
            distant(p, 2, c)
        share(p, 4, xs[p].at[core, FAR, OTHERS])
    for p in PARTS:
        gate_up(p, FAR, core)
    for p in PARTS:
        shares[p, 3].wait_recv()
        shares[p, 4].wait_recv()
        gate_up(p, FAR, other)

    lanes = lax.broadcasted_iota(jnp.int32, (256, 128), 1)
    column = lax.broadcasted_iota(jnp.int32, (256, UNITS), 1)
    for y in range(4):
        sent = x2[0, y, :, :, :, pl.ds(OUT_COLS[2], 128)].reshape(256, 128).astype(F32)
        share_of = jnp.sum(jnp.where(lax.div(lanes, 2) == tp, sent, 0.0), axis=1, keepdims=True)
        g = ga[y].reshape(256, UNITS)
        u = ua[y].reshape(256, UNITS)
        value = g / (1.0 + jnp.exp(-g)) * u
        value = value * jnp.where(column < DENSE_ROWS, 1.0, share_of)
        hid[y] = value.astype(BF).reshape(4, 4, ROWS, UNITS)

    settle()

    def hidden_rows(p, place):
        return jnp.concatenate([hid[where(p, place, i, j)] for i in range(4) for j in range(4)], axis=0)

    def pieces(p):
        return [(c, min(256, OUT_COLS[p] - c)) for c in range(0, OUT_COLS[p], 256)]

    swaps = {}

    def give(p, place):
        rows = hidden_rows(p, place)
        for c, size in pieces(p):
            piece = jnp.dot(rows, wd[other, :, pl.ds(OFFSET[p] + c, size)], preferred_element_type=F32)
            xs[p][0, place, :, :, :, pl.ds(c, size)] = piece.astype(BF).reshape(4, 4, ROWS, size)
        swaps[p, place] = send(
            xs[p].at[0, place, :, :, :, pl.ds(0, OUT_COLS[p])], rs[p].at[place],
            sum_r.at[p, place], sibling)

    def keep(p, place):
        rows = hidden_rows(p, place)
        swaps[p, place].wait_recv()
        for c, size in pieces(p):
            piece = jnp.dot(rows, wd[core, :, pl.ds(OFFSET[p] + c, size)], preferred_element_type=F32)
            theirs = rs[p][place, :, :, :, pl.ds(c, size)].reshape(256, size).astype(F32)
            os[p][place, :, :, :, pl.ds(c, size)] = (piece + theirs).astype(BF).reshape(4, 4, ROWS, size)

    def add(ref, *more):
        total = ref[...].astype(F32)
        for one in more:
            total = total + one[...].astype(F32)
        ref[...] = total.astype(BF)

    def sum_view(p, k, place, c, part=None):
        prefix = {0: (0, 0, place), 1: (0, place), 2: (place,)}[k]
        return os[p].at[(*prefix, *cut(chunks_of(k)[c], part, OUT_COLS[p]))]

    def passing_view(p, k, c, part=None):
        return passing[k, p].at[cut(chunks_of(k)[c], part, OUT_COLS[p])]

    def side_view(p, k, n, c, part=None):
        return sides[k, p].at[(n, *cut(chunks_of(k)[c], part, OUT_COLS[p]))]

    def rs_slot(k, c, n):
        return (13, 10, 0)[k] + (2 if k == 2 else 1) * c + n

    def toss(p, k, c, n, src, dst, to):
        send(src, dst, rs_r.at[p, rs_slot(k, c, n)], to[ORDER[p][k]])

    def toss_far(p, k, c):
        toss(p, k, c, 0, sum_view(p, k, FAR, c, A), passing_view(p, k, c, A), right)
        toss(p, k, c, 0, sum_view(p, k, FAR, c, B), passing_view(p, k, c, B), left)

    def toss_right(p, k, c):
        toss(p, k, c, 1, sum_view(p, k, RIGHT, c, B), side_view(p, k, 0, c, B), right)

    def toss_left(p, k, c):
        toss(p, k, c, 1, sum_view(p, k, LEFT, c, A), side_view(p, k, 1, c, A), left)

    def pass_on(p, k, c):
        landed(passing_view(p, k, c), rs_r.at[p, rs_slot(k, c, 0)])
        add(sum_view(p, k, RIGHT, c, A), passing_view(p, k, c, A))
        toss(p, k, c, 1, sum_view(p, k, RIGHT, c, A), side_view(p, k, 0, c, A), right)
        add(sum_view(p, k, LEFT, c, B), passing_view(p, k, c, B))
        toss(p, k, c, 1, sum_view(p, k, LEFT, c, B), side_view(p, k, 1, c, B), left)

    def complete(p, k, c):
        landed(side_view(p, k, slice(None), c), rs_r.at[p, rs_slot(k, c, 1)])
        add(sum_view(p, k, OWN, c), side_view(p, k, 0, c), side_view(p, k, 1, c))

    def straight(p, k):
        for n, place, to in ((0, RIGHT, right), (1, LEFT, left), (2, FAR, far)):
            toss(p, k, 0, 0, sum_view(p, k, place, 0), threes[k, p].at[n], to)

    def straight_done(p, k):
        landed(threes[k, p], rs_r.at[p, rs_slot(k, 0, 0)])
        return [threes[k, p][n] for n in range(3)]

    actions = {FAR: toss_far, RIGHT: toss_right, LEFT: toss_left}

    def produce(tasks, following):
        for n, (p, place) in enumerate(tasks):
            ahead = tasks[n + 1] if n + 1 < len(tasks) else following
            if ahead:
                give(*ahead)
            keep(p, place)
            if place in actions:
                for c in (4, 3, 1, 2, 0):
                    actions[place](p, 2, c)

    tasks = [(p, place) for place in (FAR, RIGHT, LEFT) for p in PARTS]
    give(*tasks[0])
    produce(tasks, (0, OWN))
    for p in PARTS:
        pass_on(p, 2, 4)
    for p in PARTS:
        pass_on(p, 2, 3)
    produce([(p, OWN) for p in PARTS], None)
    for p in PARTS:
        pass_on(p, 2, 1)
    for p in PARTS:
        complete(p, 2, 4)
        toss_far(p, 1, 1)
    for p in PARTS:
        pass_on(p, 2, 2)
        pass_on(p, 2, 0)
    for p in PARTS:
        complete(p, 2, 3)
        toss_right(p, 1, 1)
        toss_left(p, 1, 1)
    for p in PARTS:
        complete(p, 2, 1)
        pass_on(p, 1, 1)
    for p in PARTS:
        complete(p, 2, 2)
        straight(p, 1)
    for p in PARTS:
        complete(p, 1, 1)
        straight(p, 0)
    for p in PARTS:
        complete(p, 2, 0)
    here = []
    for p in PARTS:
        total = os[p][0, 0, 0].astype(F32)
        for one in straight_done(p, 1) + straight_done(p, 0):
            total = total + one.astype(F32)
        low, up = total[0:8], total[8:16]
        here.append(jnp.where(core == 0, low, up))
        fin_out[:, pl.ds(OFFSET[p], OUT_COLS[p])] = jnp.where(core == 0, up, low)
    last = send(fin_out, fin_in, end_r.at[1], sibling)
    for p in PARTS:
        at = pl.ds(pl.multiple_of(core * HALF + OFFSET[p], 128), OUT_COLS[p])
        out[:, at] = (tokens[:, at].astype(F32) + here[p]).astype(BF)
    last.wait_recv()
    at = pl.ds(pl.multiple_of(other * HALF, 128), HALF)
    out[:, at] = (tokens[:, at].astype(F32) + fin_in[...]).astype(BF)
    settle()
    pltpu.make_async_copy(packed.at[pl.ds(0, 31)], dbuf.at[pl.ds(0, 31)], d_s).wait()


def fused(tokens, routes, weights, packed, expert_gate, expert_up, expert_down):
    vmem = pl.BlockSpec(memory_space=pltpu.VMEM)
    hbm = pl.BlockSpec(memory_space=pl.ANY)
    cube = (4, 4, 4, ROWS)
    scratch = [pltpu.VMEM((2, *cube, IN_COLS[p]), BF) for p in PARTS]
    scratch += [pltpu.VMEM((*cube, OUT_COLS[p]), BF) for p in PARTS] * 2
    scratch += [pltpu.VMEM((*(4,) * k, ROWS, OUT_COLS[p]), BF) for k in (1, 2) for p in PARTS]
    scratch += [pltpu.VMEM((2, *(4,) * k, ROWS, OUT_COLS[p]), BF) for k in (1, 2) for p in PARTS]
    scratch += [pltpu.VMEM((3, ROWS, OUT_COLS[p]), BF) for k in (0, 1) for p in PARTS]
    scratch += [
        pltpu.VMEM((3, EXPERT_ROWS, WIDTH), BF),
        pltpu.VMEM((2, UNITS, HALF), BF),
        pltpu.VMEM((2, UNITS, HALF), BF),
        pltpu.VMEM((2, UNITS, HALF), BF),
        pltpu.VMEM((*cube, UNITS), F32),
        pltpu.VMEM((*cube, UNITS), F32),
        pltpu.VMEM((*cube, UNITS), BF),
        pltpu.VMEM((8, HALF + 128), F32),
        pltpu.VMEM((8, HALF + 128), F32),
        pltpu.VMEM((8, HALF), F32),
        pltpu.VMEM((8, HALF), F32),
        pltpu.VMEM((32, 64, 256), BF),
        pltpu.SemaphoreType.DMA((3,)),
        pltpu.SemaphoreType.DMA,
        pltpu.SemaphoreType.DMA,
        pltpu.SemaphoreType.DMA((FLIGHTS,)),
        pltpu.SemaphoreType.DMA((3, 15)),
        pltpu.SemaphoreType.DMA((3, 5)),
        pltpu.SemaphoreType.DMA((3, 14)),
        pltpu.SemaphoreType.DMA((3, 4)),
        pltpu.SemaphoreType.DMA((2,)),
    ]
    return pl.pallas_call(
        kernel,
        out_shape=jax.ShapeDtypeStruct((8, WIDTH), BF),
        in_specs=[vmem, vmem, vmem, hbm, hbm, hbm, hbm],
        out_specs=vmem,
        scratch_shapes=scratch,
        cost_estimate=pl.CostEstimate(flops=2 * 1024 * 192 * 7168 * 3, bytes_accessed=8_000_000, transcendentals=1024 * 192),
        compiler_params=pltpu.CompilerParams(
            collective_id=0, has_side_effects=True, vmem_limit_bytes=63 * 2**20),
    )(tokens, routes, weights, packed, expert_gate, expert_up, expert_down)


def per_device(tokens, routes, gate_weights, dense_gate, dense_up, dense_down, expert_gate, expert_up, expert_down):
    mains, tails = [], []
    for weight in (dense_gate, dense_up, dense_down):
        turned = weight.T
        mains.append(turned[:512].reshape(32, 16, DEPTH))
        tails.append(turned[512:].reshape(32, 4, DEPTH))
    tails.append(jnp.zeros((32, 4, DEPTH), BF))
    packed = jnp.pad(jnp.concatenate(mains + tails, axis=1), ((0, 0), (0, 0), (0, 256 - DEPTH)))
    return fused(tokens, routes.T, gate_weights.T, packed, expert_gate, expert_up, expert_down)


def solution(mesh):
    return jax.shard_map(
        per_device,
        mesh=mesh,
        in_specs=(
            P(("ep", "tp"), None),
            P(("ep", "tp"), None),
            P(("ep", "tp"), None),
            P("ep", "tp"),
            P("ep", "tp"),
            P("ep", "tp"),
            P("tp", "ep", None),
            P("tp", "ep", None),
            P("tp", "ep", None),
        ),
        out_specs=P(("ep", "tp"), None),
        check_vma=False,
    )
```

```python
import jax
import jax.numpy as jnp
from jax import lax
from jax.experimental import pallas as pl
from jax.experimental.pallas import tpu as pltpu
from jax.sharding import PartitionSpec as P

MESH = pl.DeviceIdType.MESH
BF = jnp.bfloat16
F32 = jnp.float32

WIDTH = 7168
HALF = WIDTH // 2
ROWS = 16
UNITS = 192
DENSE_ROWS = 32
EXPERT_ROWS = 152
DEPTH = 224
RUN = 4 * DEPTH
OUT_COLS = (1280, 1152, 1152)
OFFSET = (0, 1280, 2432)
IN_COLS = (1280, 1152, 1280)
CUT = 640
ORDER = (("y", "x", "z"), ("z", "y", "x"), ("x", "z", "y"))
PARTS = range(3)
OWN, RIGHT, LEFT, FAR = range(4)
BOTH = pl.ds(1, 2)
OTHERS = pl.ds(1, 3)
LINE = (0, OTHERS)
PLANE = ((0, 0), (0, OTHERS), (OTHERS, 0), (BOTH, OTHERS), (3, OTHERS))
A, B = 0, 1
FLIGHTS = 48


def cut(selected, part, cols):
    if part is None:
        return tuple(selected)
    if selected and selected[0] is BOTH:
        return (1 + part, *selected[1:])
    side = pl.ds(0, CUT) if part == A else pl.ds(CUT, cols - CUT)
    return (*selected, slice(None), side)


def view(ref, index):
    return ref.at[index] if index else ref


def kernel(
    tokens, routes, weights, dense_gate, dense_up, dense_down, expert_gate, expert_up, expert_down,
    out,
    x0, x1, x2, o0, o1, o2, r0, r1, r2,
    *rest,
):
    xs, os, rs = (x0, x1, x2), (o0, o1, o2), (r0, r1, r2)
    passing = {(k, p): rest[(k - 1) * 3 + p] for k in (1, 2) for p in PARTS}
    sides = {(k, p): rest[6 + (k - 1) * 3 + p] for k in (1, 2) for p in PARTS}
    threes = {(k, p): rest[12 + k * 3 + p] for k in (0, 1) for p in PARTS}
    rest = rest[18:]
    (raw, wg, wu, wd, ga, ua, hid, tok_out, tok_in, fin_out, fin_in, packed, dbuf,
     w_sem, d_s, d_r, out_s, ag_r, sib_r, rs_r, sum_r, end_r) = rest

    ep, tp = lax.axis_index("ep"), lax.axis_index("tp")
    core = lax.rem(tp, 2)
    other = 1 - core
    pos = {
        "x": lax.div(ep, 8),
        "y": lax.div(tp, 2) * 2 + lax.rem(lax.div(ep, 4), 2),
        "z": lax.rem(ep, 4),
    }

    def device(x, y, z):
        return {"ep": x * 8 + lax.rem(y, 2) * 4 + z, "tp": lax.div(y, 2) * 2 + core}

    def moved(axis, by):
        place = dict(pos)
        place[axis] = lax.rem(pos[axis] + by, 4)
        return device(place["x"], place["y"], place["z"])

    right = {a: moved(a, 1) for a in "xyz"}
    left = {a: moved(a, 3) for a in "xyz"}
    far = {a: moved(a, 2) for a in "xyz"}
    sibling = {"ep": ep, "tp": lax.div(tp, 2) * 2 + other}

    loads = [
        pltpu.make_async_copy(w.at[0], raw.at[n], w_sem.at[n])
        for n, w in enumerate((expert_gate, expert_up, expert_down))
    ]
    for load in loads:
        load.start()

    y_low = lax.rem(pos["y"], 2)
    steps = sorted(
        ((dx, dy, dz) for dx in range(4) for dy in range(2) for dz in range(4) if dx or dy or dz),
        key=lambda d: min(d[0], 4 - d[0]) + d[1] + min(d[2], 4 - d[2]))

    def peer(dx, dy, dz):
        return lax.rem(pos["x"] + dx, 4) * 8 + lax.rem(y_low + dy, 2) * 4 + lax.rem(pos["z"] + dz, 4)

    peers = [peer(*d) for d in steps]

    barrier = pltpu.get_barrier_semaphore()
    pl.semaphore_signal(barrier, inc=1, device_id=sibling, device_id_type=MESH)
    for by in (1, 2, 3):
        pl.semaphore_signal(barrier, inc=1, device_id=moved("y", by), device_id_type=MESH)
    for d, to in zip(steps, peers):
        if d != (0, 1, 0):
            pl.semaphore_signal(barrier, inc=1, device_id={"ep": to, "tp": tp}, device_id_type=MESH)
    pl.semaphore_wait(barrier, 34)

    flying = []

    def send(src, dst, r_sem, to):
        n = len(flying)
        if n >= FLIGHTS:
            flying[n - FLIGHTS].wait_send()
        copy = pltpu.make_async_remote_copy(
            src_ref=src, dst_ref=dst, send_sem=out_s.at[n % FLIGHTS], recv_sem=r_sem, device_id=to, device_id_type=MESH)
        copy.start()
        flying.append(copy)
        return copy

    def settle():
        for copy in flying[max(0, len(flying) - FLIGHTS):]:
            copy.wait_send()
        flying.clear()

    def landed(ref, sem):
        pltpu.make_async_copy(ref, ref, sem).wait()

    diagonal = lax.broadcasted_iota(jnp.int32, (8, 8), 0) == lax.broadcasted_iota(jnp.int32, (8, 8), 1)

    def column_of(row):
        return jnp.sum(jnp.where(diagonal, jnp.broadcast_to(row, (8, 8)), jnp.zeros((8, 8), row.dtype)), axis=1, keepdims=True)

    lane = lax.broadcasted_iota(jnp.int32, (8, 128), 1)
    named = lax.div(lane, 2).astype(F32)
    chosen = [column_of(routes[n:n + 1, :].astype(F32)) for n in range(2)]
    factor = jnp.where(chosen[0] == named, column_of(weights[0:1, :]), 0.0) + jnp.where(
        chosen[1] == named, column_of(weights[1:2, :]), 0.0)
    high = factor.astype(BF).astype(F32)
    factor = jnp.where(lax.rem(lane, 2) == 0, high, factor - high)
    tok_out[:, pl.ds(0, HALF)] = tokens[:, pl.ds(pl.multiple_of(other * HALF, 128), HALF)].astype(F32)
    tok_out[:, pl.ds(HALF, 128)] = factor
    swap = send(tok_out, tok_in, end_r.at[0], sibling)
    swap.wait_recv()
    for p in PARTS:
        mine = tokens[:, pl.ds(pl.multiple_of(core * HALF + OFFSET[p], 128), OUT_COLS[p])].astype(F32)
        if IN_COLS[p] > OUT_COLS[p]:
            mine = jnp.concatenate([mine, factor], axis=1)
        theirs = tok_in[:, pl.ds(OFFSET[p], IN_COLS[p])]
        first = jnp.where(core == 0, mine, theirs)
        second = jnp.where(core == 0, theirs, mine)
        xs[p][core, 0, 0, 0] = jnp.concatenate([first, second], axis=0).astype(BF)

    def chunks_of(k):
        return ((),) if k == 0 else tuple((s,) for s in LINE) if k == 1 else PLANE

    def token_view(p, k, place, c, part=None):
        prefix = {0: (core, 0, 0, place), 1: (core, 0, place), 2: (core, place)}[k]
        return xs[p].at[(*prefix, *cut(chunks_of(k)[c], part, IN_COLS[p]))]

    def ag_slot(k, c, n):
        return 0 if k == 0 else (0, 1, 5)[k] + 2 * c + n

    def fly(p, k, c, n, src, dst, to):
        send(src, dst, ag_r.at[p, ag_slot(k, c, n)], to[ORDER[p][k]])

    def spread(p, k, c=0, direct=False):
        own = token_view(p, k, OWN, c)
        fly(p, k, c, 0, own, token_view(p, k, LEFT, c), right)
        fly(p, k, c, 0, own, token_view(p, k, RIGHT, c), left)
        if direct:
            fly(p, k, c, 1, own, token_view(p, k, FAR, c), far)

    def near(p, k, c=0):
        landed(token_view(p, k, OTHERS if k == 0 else BOTH, c), ag_r.at[p, ag_slot(k, c, 0)])

    def relay(p, k, c=0):
        near(p, k, c)
        fly(p, k, c, 1, token_view(p, k, LEFT, c, A), token_view(p, k, FAR, c, A), right)
        fly(p, k, c, 1, token_view(p, k, RIGHT, c, B), token_view(p, k, FAR, c, B), left)

    def distant(p, k, c=0):
        landed(token_view(p, k, FAR, c), ag_r.at[p, ag_slot(k, c, 1)])

    shares = {}

    def share(p, n, ref):
        shares[p, n] = send(ref, ref, sib_r.at[p, n], sibling)

    def where(p, third, second, first):
        place = dict(zip(ORDER[p], (first, second, third)))
        return place["y"], place["z"], place["x"]

    def gate_up(p, place, h):
        cols = OUT_COLS[p]
        rows = xs[p][h, place, :, :, :, pl.ds(0, cols)].reshape(256, cols)
        for w, acc in ((wg, ga), (wu, ua)):
            piece = lax.dot_general(
                rows, w[h, :, pl.ds(OFFSET[p], cols)], (((1,), (1,)), ((), ())), preferred_element_type=F32)
            for i in range(4):
                for j in range(4):
                    n = (i * 4 + j) * ROWS
                    acc[where(p, place, i, j)] += piece[n:n + ROWS]

    def dense_pack():
        tails = []
        for n, w in enumerate((dense_gate, dense_up, dense_down)):
            rows = jnp.concatenate([w[...].astype(F32), jnp.zeros((256 - DEPTH, 640), F32)], axis=0)
            turned = rows.T.astype(BF)
            packed[:, pl.ds(16 * n, 16), :] = turned[:512].reshape(32, 16, 256)
            tails.append(turned[512:])
        place = lax.broadcasted_iota(jnp.int32, (512, 384), 0)
        unit = lax.broadcasted_iota(jnp.int32, (512, 384), 1)
        to, row = lax.div(place, 16), lax.rem(place, 16)
        wanted = lax.div(row, 4) * 128 + to * 4 + lax.rem(row, 4)
        pick = jnp.where(unit == wanted, 1.0, 0.0).astype(BF)
        moved_rows = jnp.dot(pick, jnp.concatenate(tails, axis=0), preferred_element_type=F32)
        packed[:, pl.ds(48, 16), :] = moved_rows.astype(BF).reshape(32, 16, 256)
        pltpu.make_async_copy(packed.at[ep], dbuf.at[ep], d_r).start()

    def dense_out(first, last):
        for to in peers[first:last]:
            pltpu.make_async_remote_copy(
                src_ref=packed.at[to], dst_ref=dbuf.at[ep], send_sem=d_s, recv_sem=d_r,
                device_id={"ep": to, "tp": tp}, device_id_type=MESH).start()

    def dense_in():
        landed(dbuf, d_r)
        row = lax.broadcasted_iota(jnp.int32, (ROWS, RUN), 0)
        for i in range(8):
            at = pl.ds((i % 4) * RUN, RUN)
            run = jnp.concatenate([dbuf[4 * i + z][:, 0:DEPTH].astype(F32) for z in range(4)], axis=1)
            tail = run[48:64]
            for n, w in enumerate((wg, wu, wd)):
                w[i // 4, pl.ds(0, 16), at] = run[16 * n:16 * n + 16].astype(BF)
                turned = tail if n == 0 else pltpu.roll(tail, 16 - 4 * n, 0)
                w[i // 4, pl.ds(16, 16), at] = jnp.where(row < 4, turned, 0.0).astype(BF)

    def expert_in():
        for load in loads[:3]:
            load.wait()
        for n, w in enumerate((wg, wu, wd)):
            for h in range(2):
                w[h, pl.ds(176, 16)] = jnp.zeros((16, HALF), BF)
                w[h, pl.ds(DENSE_ROWS, EXPERT_ROWS)] = raw[n, :, pl.ds(h * HALF, HALF)]
        ga[...] = jnp.zeros_like(ga)
        ua[...] = jnp.zeros_like(ua)

    for p in PARTS:
        spread(p, 0, direct=True)
    for p in PARTS:
        spread(p, 1, 0, direct=True)
    for p in PARTS:
        spread(p, 2, 0)
    dense_pack()
    dense_out(0, 16)
    for p in PARTS:
        near(p, 0)
        spread(p, 1, 1)
        spread(p, 2, 1)
    dense_out(16, 24)
    for p in PARTS:
        near(p, 1, 0)
        distant(p, 1, 0)
        spread(p, 2, 2)
    dense_out(24, 31)
    for p in PARTS:
        relay(p, 2, 0)
    for p in PARTS:
        relay(p, 1, 1)
        spread(p, 2, 3)
    for p in PARTS:
        distant(p, 1, 1)
        spread(p, 2, 4)
        share(p, 0, xs[p].at[core, 0])
    expert_in()
    for p in PARTS:
        relay(p, 2, 1)
    for p in PARTS:
        relay(p, 2, 2)
    dense_in()
    for p in PARTS:
        relay(p, 2, 3)
    for p in PARTS:
        gate_up(p, OWN, core)
    for p in PARTS:
        relay(p, 2, 4)
        share(p, 1, xs[p].at[core, RIGHT])
        share(p, 2, xs[p].at[core, LEFT])
    for p in PARTS:
        shares[p, 0].wait_recv()
        gate_up(p, OWN, other)
    for p in PARTS:
        gate_up(p, RIGHT, core)
        gate_up(p, LEFT, core)
    for p in PARTS:
        for c in (0, 1):
            distant(p, 2, c)
        share(p, 3, xs[p].at[core, FAR, 0])
    for p in PARTS:
        shares[p, 1].wait_recv()
        gate_up(p, RIGHT, other)
        shares[p, 2].wait_recv()
        gate_up(p, LEFT, other)
    for p in PARTS:
        for c in (2, 3, 4):
            distant(p, 2, c)
        share(p, 4, xs[p].at[core, FAR, OTHERS])
    for p in PARTS:
        gate_up(p, FAR, core)
    for p in PARTS:
        shares[p, 3].wait_recv()
        shares[p, 4].wait_recv()
        gate_up(p, FAR, other)

    lanes = lax.broadcasted_iota(jnp.int32, (256, 128), 1)
    column = lax.broadcasted_iota(jnp.int32, (256, UNITS), 1)
    for y in range(4):
        sent = x2[0, y, :, :, :, pl.ds(OUT_COLS[2], 128)].reshape(256, 128).astype(F32)
        share_of = jnp.sum(jnp.where(lax.div(lanes, 2) == tp, sent, 0.0), axis=1, keepdims=True)
        g = ga[y].reshape(256, UNITS)
        u = ua[y].reshape(256, UNITS)
        value = g / (1.0 + jnp.exp(-g)) * u
        value = value * jnp.where(column < DENSE_ROWS, 1.0, share_of)
        hid[y] = value.astype(BF).reshape(4, 4, ROWS, UNITS)

    settle()

    def hidden_rows(p, place):
        return jnp.concatenate([hid[where(p, place, i, j)] for i in range(4) for j in range(4)], axis=0)

    def pieces(p):
        return [(c, min(256, OUT_COLS[p] - c)) for c in range(0, OUT_COLS[p], 256)]

    swaps = {}

    def give(p, place):
        rows = hidden_rows(p, place)
        for c, size in pieces(p):
            piece = jnp.dot(rows, wd[other, :, pl.ds(OFFSET[p] + c, size)], preferred_element_type=F32)
            xs[p][0, place, :, :, :, pl.ds(c, size)] = piece.astype(BF).reshape(4, 4, ROWS, size)
        swaps[p, place] = send(
            xs[p].at[0, place, :, :, :, pl.ds(0, OUT_COLS[p])], rs[p].at[place],
            sum_r.at[p, place], sibling)

    def keep(p, place):
        rows = hidden_rows(p, place)
        swaps[p, place].wait_recv()
        for c, size in pieces(p):
            piece = jnp.dot(rows, wd[core, :, pl.ds(OFFSET[p] + c, size)], preferred_element_type=F32)
            theirs = rs[p][place, :, :, :, pl.ds(c, size)].reshape(256, size).astype(F32)
            os[p][place, :, :, :, pl.ds(c, size)] = (piece + theirs).astype(BF).reshape(4, 4, ROWS, size)

    def add(ref, *more):
        total = ref[...].astype(F32)
        for one in more:
            total = total + one[...].astype(F32)
        ref[...] = total.astype(BF)

    def sum_view(p, k, place, c, part=None):
        prefix = {0: (0, 0, place), 1: (0, place), 2: (place,)}[k]
        return os[p].at[(*prefix, *cut(chunks_of(k)[c], part, OUT_COLS[p]))]

    def passing_view(p, k, c, part=None):
        return passing[k, p].at[cut(chunks_of(k)[c], part, OUT_COLS[p])]

    def side_view(p, k, n, c, part=None):
        return sides[k, p].at[(n, *cut(chunks_of(k)[c], part, OUT_COLS[p]))]

    def rs_slot(k, c, n):
        return (13, 10, 0)[k] + (2 if k == 2 else 1) * c + n

    def toss(p, k, c, n, src, dst, to):
        send(src, dst, rs_r.at[p, rs_slot(k, c, n)], to[ORDER[p][k]])

    def toss_far(p, k, c):
        toss(p, k, c, 0, sum_view(p, k, FAR, c, A), passing_view(p, k, c, A), right)
        toss(p, k, c, 0, sum_view(p, k, FAR, c, B), passing_view(p, k, c, B), left)

    def toss_right(p, k, c):
        toss(p, k, c, 1, sum_view(p, k, RIGHT, c, B), side_view(p, k, 0, c, B), right)

    def toss_left(p, k, c):
        toss(p, k, c, 1, sum_view(p, k, LEFT, c, A), side_view(p, k, 1, c, A), left)

    def pass_on(p, k, c):
        landed(passing_view(p, k, c), rs_r.at[p, rs_slot(k, c, 0)])
        add(sum_view(p, k, RIGHT, c, A), passing_view(p, k, c, A))
        toss(p, k, c, 1, sum_view(p, k, RIGHT, c, A), side_view(p, k, 0, c, A), right)
        add(sum_view(p, k, LEFT, c, B), passing_view(p, k, c, B))
        toss(p, k, c, 1, sum_view(p, k, LEFT, c, B), side_view(p, k, 1, c, B), left)

    def complete(p, k, c):
        landed(side_view(p, k, slice(None), c), rs_r.at[p, rs_slot(k, c, 1)])
        add(sum_view(p, k, OWN, c), side_view(p, k, 0, c), side_view(p, k, 1, c))

    def straight(p, k):
        for n, place, to in ((0, RIGHT, right), (1, LEFT, left), (2, FAR, far)):
            toss(p, k, 0, 0, sum_view(p, k, place, 0), threes[k, p].at[n], to)

    def straight_done(p, k):
        landed(threes[k, p], rs_r.at[p, rs_slot(k, 0, 0)])
        return [threes[k, p][n] for n in range(3)]

    actions = {FAR: toss_far, RIGHT: toss_right, LEFT: toss_left}

    def produce(tasks, following):
        for n, (p, place) in enumerate(tasks):
            ahead = tasks[n + 1] if n + 1 < len(tasks) else following
            if ahead:
                give(*ahead)
            keep(p, place)
            if place in actions:
                for c in (4, 3, 1, 2, 0):
                    actions[place](p, 2, c)

    tasks = [(p, place) for place in (FAR, RIGHT, LEFT) for p in PARTS]
    give(*tasks[0])
    produce(tasks, (0, OWN))
    for p in PARTS:
        pass_on(p, 2, 4)
    for p in PARTS:
        pass_on(p, 2, 3)
    produce([(p, OWN) for p in PARTS], None)
    for p in PARTS:
        pass_on(p, 2, 1)
    for p in PARTS:
        complete(p, 2, 4)
        toss_far(p, 1, 1)
    for p in PARTS:
        pass_on(p, 2, 2)
        pass_on(p, 2, 0)
    for p in PARTS:
        complete(p, 2, 3)
        toss_right(p, 1, 1)
        toss_left(p, 1, 1)
    for p in PARTS:
        complete(p, 2, 1)
        pass_on(p, 1, 1)
    for p in PARTS:
        complete(p, 2, 2)
        straight(p, 1)
    for p in PARTS:
        complete(p, 1, 1)
        straight(p, 0)
    for p in PARTS:
        complete(p, 2, 0)
    here = []
    for p in PARTS:
        total = os[p][0, 0, 0].astype(F32)
        for one in straight_done(p, 1) + straight_done(p, 0):
            total = total + one.astype(F32)
        low, up = total[0:8], total[8:16]
        here.append(jnp.where(core == 0, low, up))
        fin_out[:, pl.ds(OFFSET[p], OUT_COLS[p])] = jnp.where(core == 0, up, low)
    last = send(fin_out, fin_in, end_r.at[1], sibling)
    for p in PARTS:
        at = pl.ds(pl.multiple_of(core * HALF + OFFSET[p], 128), OUT_COLS[p])
        out[:, at] = (tokens[:, at].astype(F32) + here[p]).astype(BF)
    last.wait_recv()
    at = pl.ds(pl.multiple_of(other * HALF, 128), HALF)
    out[:, at] = (tokens[:, at].astype(F32) + fin_in[...]).astype(BF)
    settle()
    pltpu.make_async_copy(packed.at[pl.ds(0, 31)], dbuf.at[pl.ds(0, 31)], d_s).wait()


def fused(tokens, routes, weights, dense_gate, dense_up, dense_down, expert_gate, expert_up, expert_down):
    vmem = pl.BlockSpec(memory_space=pltpu.VMEM)
    hbm = pl.BlockSpec(memory_space=pl.ANY)
    cube = (4, 4, 4, ROWS)
    scratch = [pltpu.VMEM((2, *cube, IN_COLS[p]), BF) for p in PARTS]
    scratch += [pltpu.VMEM((*cube, OUT_COLS[p]), BF) for p in PARTS] * 2
    scratch += [pltpu.VMEM((*(4,) * k, ROWS, OUT_COLS[p]), BF) for k in (1, 2) for p in PARTS]
    scratch += [pltpu.VMEM((2, *(4,) * k, ROWS, OUT_COLS[p]), BF) for k in (1, 2) for p in PARTS]
    scratch += [pltpu.VMEM((3, ROWS, OUT_COLS[p]), BF) for k in (0, 1) for p in PARTS]
    scratch += [
        pltpu.VMEM((3, EXPERT_ROWS, WIDTH), BF),
        pltpu.VMEM((2, UNITS, HALF), BF),
        pltpu.VMEM((2, UNITS, HALF), BF),
        pltpu.VMEM((2, UNITS, HALF), BF),
        pltpu.VMEM((*cube, UNITS), F32),
        pltpu.VMEM((*cube, UNITS), F32),
        pltpu.VMEM((*cube, UNITS), BF),
        pltpu.VMEM((8, HALF + 128), F32),
        pltpu.VMEM((8, HALF + 128), F32),
        pltpu.VMEM((8, HALF), F32),
        pltpu.VMEM((8, HALF), F32),
        pltpu.VMEM((32, 64, 256), BF),
        pltpu.VMEM((32, 64, 256), BF),
        pltpu.SemaphoreType.DMA((3,)),
        pltpu.SemaphoreType.DMA,
        pltpu.SemaphoreType.DMA,
        pltpu.SemaphoreType.DMA((FLIGHTS,)),
        pltpu.SemaphoreType.DMA((3, 15)),
        pltpu.SemaphoreType.DMA((3, 5)),
        pltpu.SemaphoreType.DMA((3, 14)),
        pltpu.SemaphoreType.DMA((3, 4)),
        pltpu.SemaphoreType.DMA((2,)),
    ]
    return pl.pallas_call(
        kernel,
        out_shape=jax.ShapeDtypeStruct((8, WIDTH), BF),
        in_specs=[vmem] * 6 + [hbm] * 3,
        out_specs=vmem,
        scratch_shapes=scratch,
        cost_estimate=pl.CostEstimate(flops=2 * 1024 * 192 * 7168 * 3, bytes_accessed=8_000_000, transcendentals=1024 * 192),
        compiler_params=pltpu.CompilerParams(
            collective_id=0, has_side_effects=True, vmem_limit_bytes=63 * 2**20),
    )(tokens, routes, weights, dense_gate, dense_up, dense_down, expert_gate, expert_up, expert_down)


def per_device(tokens, routes, gate_weights, dense_gate, dense_up, dense_down, expert_gate, expert_up, expert_down):
    return fused(
        tokens, routes.T, gate_weights.T, dense_gate, dense_up, dense_down, expert_gate, expert_up, expert_down)


def solution(mesh):
    return jax.shard_map(
        per_device,
        mesh=mesh,
        in_specs=(
            P(("ep", "tp"), None),
            P(("ep", "tp"), None),
            P(("ep", "tp"), None),
            P("ep", "tp"),
            P("ep", "tp"),
            P("ep", "tp"),
            P("tp", "ep", None),
            P("tp", "ep", None),
            P("tp", "ep", None),
        ),
        out_specs=P(("ep", "tp"), None),
        check_vma=False,
    )
```

```python
import jax
import jax.numpy as jnp
from jax import lax
from jax.experimental import pallas as pl
from jax.experimental.pallas import tpu as pltpu
from jax.sharding import PartitionSpec as P

MESH = pl.DeviceIdType.MESH
BF = jnp.bfloat16
F32 = jnp.float32

WIDTH = 7168
HALF = WIDTH // 2
ROWS = 16
UNITS = 192
DENSE_ROWS = 32
EXPERT_ROWS = 152
DEPTH = 224
RUN = 4 * DEPTH
OUT_COLS = (1280, 1152, 1152)
OFFSET = (0, 1280, 2432)
IN_COLS = (1280, 1152, 1280)
CUT = 640
ORDER = (("y", "x", "z"), ("z", "y", "x"), ("x", "z", "y"))
PARTS = range(3)
OWN, RIGHT, LEFT, FAR = range(4)
BOTH = pl.ds(1, 2)
OTHERS = pl.ds(1, 3)
LINE = (0, OTHERS)
PLANE = ((0, 0), (0, OTHERS), (OTHERS, 0), (BOTH, OTHERS), (3, OTHERS))
A, B = 0, 1
LEAD = 3
FLIGHTS = 48


def cut(selected, part, cols):
    if part is None:
        return tuple(selected)
    side = pl.ds(0, CUT) if part == A else pl.ds(CUT, cols - CUT)
    return (*selected, slice(None), side)


def view(ref, index):
    return ref.at[index] if index else ref


def kernel(
    tokens, routes, weights, dense_gate, dense_up, dense_down, expert_gate, expert_up, expert_down,
    out,
    x0, x1, x2, o0, o1, o2, r0, r1, r2,
    *rest,
):
    xs, os, rs = (x0, x1, x2), (o0, o1, o2), (r0, r1, r2)
    passing = {(k, p): rest[(k - 1) * 3 + p] for k in (1, 2) for p in PARTS}
    sides = {(k, p): rest[6 + (k - 1) * 3 + p] for k in (1, 2) for p in PARTS}
    threes = {(k, p): rest[12 + k * 3 + p] for k in (0, 1) for p in PARTS}
    rest = rest[18:]
    (raw, wg, wu, wd, ga, ua, hid, tok_out, tok_in, fin_out, fin_in, packed, dbuf,
     w_sem, d_s, d_r, out_s, ag_r, sib_r, rs_r, sum_r, end_r) = rest

    ep, tp = lax.axis_index("ep"), lax.axis_index("tp")
    core = lax.rem(tp, 2)
    other = 1 - core
    pos = {
        "x": lax.div(ep, 8),
        "y": lax.div(tp, 2) * 2 + lax.rem(lax.div(ep, 4), 2),
        "z": lax.rem(ep, 4),
    }

    def device(x, y, z):
        return {"ep": x * 8 + lax.rem(y, 2) * 4 + z, "tp": lax.div(y, 2) * 2 + core}

    def moved(axis, by):
        place = dict(pos)
        place[axis] = lax.rem(pos[axis] + by, 4)
        return device(place["x"], place["y"], place["z"])

    right = {a: moved(a, 1) for a in "xyz"}
    left = {a: moved(a, 3) for a in "xyz"}
    far = {a: moved(a, 2) for a in "xyz"}
    sibling = {"ep": ep, "tp": lax.div(tp, 2) * 2 + other}

    loads = [
        pltpu.make_async_copy(w.at[0], raw.at[n], w_sem.at[n])
        for n, w in enumerate((expert_gate, expert_up, expert_down))
    ]
    for load in loads:
        load.start()

    y_low = lax.rem(pos["y"], 2)
    steps = sorted(
        ((dx, dy, dz) for dx in range(4) for dy in range(2) for dz in range(4) if dx or dy or dz),
        key=lambda d: min(d[0], 4 - d[0]) + d[1] + min(d[2], 4 - d[2]))

    def peer(dx, dy, dz):
        return lax.rem(pos["x"] + dx, 4) * 8 + lax.rem(y_low + dy, 2) * 4 + lax.rem(pos["z"] + dz, 4)

    peers = [peer(*d) for d in steps]

    barrier = pltpu.get_barrier_semaphore()
    pl.semaphore_signal(barrier, inc=1, device_id=sibling, device_id_type=MESH)
    for by in (1, 2, 3):
        pl.semaphore_signal(barrier, inc=1, device_id=moved("y", by), device_id_type=MESH)
    for d, to in zip(steps, peers):
        if d != (0, 1, 0):
            pl.semaphore_signal(barrier, inc=1, device_id={"ep": to, "tp": tp}, device_id_type=MESH)
    pl.semaphore_wait(barrier, 34)

    flying = []

    def send(src, dst, r_sem, to):
        n = len(flying)
        if n >= FLIGHTS:
            flying[n - FLIGHTS].wait_send()
        copy = pltpu.make_async_remote_copy(
            src_ref=src, dst_ref=dst, send_sem=out_s.at[n % FLIGHTS], recv_sem=r_sem, device_id=to, device_id_type=MESH)
        copy.start()
        flying.append(copy)
        return copy

    def settle():
        for copy in flying[max(0, len(flying) - FLIGHTS):]:
            copy.wait_send()
        flying.clear()

    def landed(ref, sem):
        pltpu.make_async_copy(ref, ref, sem).wait()

    diagonal = lax.broadcasted_iota(jnp.int32, (8, 8), 0) == lax.broadcasted_iota(jnp.int32, (8, 8), 1)

    def column_of(row):
        return jnp.sum(jnp.where(diagonal, jnp.broadcast_to(row, (8, 8)), jnp.zeros((8, 8), row.dtype)), axis=1, keepdims=True)

    lane = lax.broadcasted_iota(jnp.int32, (8, 128), 1)
    named = lax.div(lane, 2).astype(F32)
    chosen = [column_of(routes[n:n + 1, :].astype(F32)) for n in range(2)]
    factor = jnp.where(chosen[0] == named, column_of(weights[0:1, :]), 0.0) + jnp.where(
        chosen[1] == named, column_of(weights[1:2, :]), 0.0)
    high = factor.astype(BF).astype(F32)
    factor = jnp.where(lax.rem(lane, 2) == 0, high, factor - high)
    tok_out[:, pl.ds(0, HALF)] = tokens[:, pl.ds(pl.multiple_of(other * HALF, 128), HALF)].astype(F32)
    tok_out[:, pl.ds(HALF, 128)] = factor
    swap = send(tok_out, tok_in, end_r.at[0], sibling)
    swap.wait_recv()
    for p in PARTS:
        mine = tokens[:, pl.ds(pl.multiple_of(core * HALF + OFFSET[p], 128), OUT_COLS[p])].astype(F32)
        if IN_COLS[p] > OUT_COLS[p]:
            mine = jnp.concatenate([mine, factor], axis=1)
        theirs = tok_in[:, pl.ds(OFFSET[p], IN_COLS[p])]
        first = jnp.where(core == 0, mine, theirs)
        second = jnp.where(core == 0, theirs, mine)
        xs[p][core, 0, 0, 0] = jnp.concatenate([first, second], axis=0).astype(BF)

    def chunks_of(k):
        return ((),) if k == 0 else tuple((s,) for s in LINE) if k == 1 else PLANE

    def token_view(p, k, place, c, part=None):
        prefix = {0: (core, 0, 0, place), 1: (core, 0, place), 2: (core, place)}[k]
        return xs[p].at[(*prefix, *cut(chunks_of(k)[c], part, IN_COLS[p]))]

    def ag_slot(k, c, n):
        return 0 if k == 0 else (0, 1, 5)[k] + 2 * c + n

    def fly(p, k, c, n, src, dst, to):
        send(src, dst, ag_r.at[p, ag_slot(k, c, n)], to[ORDER[p][k]])

    def spread(p, k, c=0, direct=False):
        own = token_view(p, k, OWN, c)
        fly(p, k, c, 0, own, token_view(p, k, LEFT, c), right)
        fly(p, k, c, 0, own, token_view(p, k, RIGHT, c), left)
        if direct:
            fly(p, k, c, 1, own, token_view(p, k, FAR, c), far)

    def near(p, k, c=0):
        landed(token_view(p, k, OTHERS if k == 0 else BOTH, c), ag_r.at[p, ag_slot(k, c, 0)])

    def relay(p, k, c=0):
        near(p, k, c)
        fly(p, k, c, 1, token_view(p, k, LEFT, c, A), token_view(p, k, FAR, c, A), right)
        fly(p, k, c, 1, token_view(p, k, RIGHT, c, B), token_view(p, k, FAR, c, B), left)

    def distant(p, k, c=0):
        landed(token_view(p, k, FAR, c), ag_r.at[p, ag_slot(k, c, 1)])

    shares = {}

    def share(p, n, ref):
        shares[p, n] = send(ref, ref, sib_r.at[p, n], sibling)

    def where(p, third, second, first):
        place = dict(zip(ORDER[p], (first, second, third)))
        return place["y"], place["z"], place["x"]

    def gate_up(p, place, h):
        cols = OUT_COLS[p]
        rows = xs[p][h, place, :, :, :, pl.ds(0, cols)].reshape(256, cols)
        for w, acc in ((wg, ga), (wu, ua)):
            piece = lax.dot_general(
                rows, w[h, :, pl.ds(OFFSET[p], cols)], (((1,), (1,)), ((), ())), preferred_element_type=F32)
            for i in range(4):
                for j in range(4):
                    n = (i * 4 + j) * ROWS
                    acc[where(p, place, i, j)] += piece[n:n + ROWS]

    def dense_pack():
        tails = []
        for n, w in enumerate((dense_gate, dense_up, dense_down)):
            rows = jnp.concatenate([w[...].astype(F32), jnp.zeros((256 - DEPTH, 640), F32)], axis=0)
            turned = rows.T.astype(BF)
            packed[:, pl.ds(16 * n, 16), :] = turned[:512].reshape(32, 16, 256)
            tails.append(turned[512:])
        place = lax.broadcasted_iota(jnp.int32, (512, 384), 0)
        unit = lax.broadcasted_iota(jnp.int32, (512, 384), 1)
        to, row = lax.div(place, 16), lax.rem(place, 16)
        wanted = lax.div(row, 4) * 128 + to * 4 + lax.rem(row, 4)
        pick = jnp.where(unit == wanted, 1.0, 0.0).astype(BF)
        moved_rows = jnp.dot(pick, jnp.concatenate(tails, axis=0), preferred_element_type=F32)
        packed[:, pl.ds(48, 16), :] = moved_rows.astype(BF).reshape(32, 16, 256)
        pltpu.make_async_copy(packed.at[ep], dbuf.at[ep], d_r).start()

    def dense_out(first, last):
        for to in peers[first:last]:
            pltpu.make_async_remote_copy(
                src_ref=packed.at[to], dst_ref=dbuf.at[ep], send_sem=d_s, recv_sem=d_r,
                device_id={"ep": to, "tp": tp}, device_id_type=MESH).start()

    def dense_in():
        landed(dbuf, d_r)
        row = lax.broadcasted_iota(jnp.int32, (ROWS, RUN), 0)
        for i in range(8):
            at = pl.ds((i % 4) * RUN, RUN)
            run = jnp.concatenate([dbuf[4 * i + z][:, 0:DEPTH].astype(F32) for z in range(4)], axis=1)
            tail = run[48:64]
            for n, w in enumerate((wg, wu, wd)):
                w[i // 4, pl.ds(0, 16), at] = run[16 * n:16 * n + 16].astype(BF)
                turned = tail if n == 0 else pltpu.roll(tail, 16 - 4 * n, 0)
                w[i // 4, pl.ds(16, 16), at] = jnp.where(row < 4, turned, 0.0).astype(BF)

    def expert_in():
        for load in loads[:3]:
            load.wait()
        for n, w in enumerate((wg, wu, wd)):
            for h in range(2):
                w[h, pl.ds(176, 16)] = jnp.zeros((16, HALF), BF)
                w[h, pl.ds(DENSE_ROWS, EXPERT_ROWS)] = raw[n, :, pl.ds(h * HALF, HALF)]
        ga[...] = jnp.zeros_like(ga)
        ua[...] = jnp.zeros_like(ua)

    for p in PARTS:
        spread(p, 0, direct=True)
    for p in PARTS:
        spread(p, 1, 0, direct=True)
    for p in PARTS:
        spread(p, 2, 0)
    dense_pack()
    dense_out(0, 16)
    for p in PARTS:
        near(p, 0)
        spread(p, 1, 1, direct=True)
        spread(p, 2, 1)
    dense_out(16, 24)
    for p in PARTS:
        near(p, 1, 0)
        distant(p, 1, 0)
        spread(p, 2, 2)
    dense_out(24, 31)
    for p in PARTS:
        relay(p, 2, 0)
    for p in PARTS:
        near(p, 1, 1)
        spread(p, 2, 3)
    for p in PARTS:
        distant(p, 1, 1)
        spread(p, 2, 4)
        share(p, 0, xs[p].at[core, 0])
    expert_in()
    for p in PARTS:
        relay(p, 2, 1)
    for p in PARTS:
        relay(p, 2, 2)
    dense_in()
    for p in PARTS:
        relay(p, 2, 3)
    for p in PARTS:
        gate_up(p, OWN, core)
    for p in PARTS:
        relay(p, 2, 4)
        share(p, 1, xs[p].at[core, RIGHT])
        share(p, 2, xs[p].at[core, LEFT])
    for p in PARTS:
        shares[p, 0].wait_recv()
        gate_up(p, OWN, other)
    for p in PARTS:
        gate_up(p, RIGHT, core)
        gate_up(p, LEFT, core)
    for p in PARTS:
        for c in (0, 1):
            distant(p, 2, c)
        share(p, 3, xs[p].at[core, FAR, 0])
    for p in PARTS:
        shares[p, 1].wait_recv()
        gate_up(p, RIGHT, other)
        shares[p, 2].wait_recv()
        gate_up(p, LEFT, other)
    for p in PARTS:
        for c in (2, 3, 4):
            distant(p, 2, c)
        share(p, 4, xs[p].at[core, FAR, OTHERS])
    for p in PARTS:
        gate_up(p, FAR, core)
    for p in PARTS:
        shares[p, 3].wait_recv()
        shares[p, 4].wait_recv()
        gate_up(p, FAR, other)

    lanes = lax.broadcasted_iota(jnp.int32, (256, 128), 1)
    column = lax.broadcasted_iota(jnp.int32, (256, UNITS), 1)
    for y in range(4):
        sent = x2[0, y, :, :, :, pl.ds(OUT_COLS[2], 128)].reshape(256, 128).astype(F32)
        share_of = jnp.sum(jnp.where(lax.div(lanes, 2) == tp, sent, 0.0), axis=1, keepdims=True)
        g = ga[y].reshape(256, UNITS)
        u = ua[y].reshape(256, UNITS)
        value = g / (1.0 + jnp.exp(-g)) * u
        value = value * jnp.where(column < DENSE_ROWS, 1.0, share_of)
        hid[y] = value.astype(BF).reshape(4, 4, ROWS, UNITS)

    settle()

    def hidden_rows(p, place):
        return jnp.concatenate([hid[where(p, place, i, j)] for i in range(4) for j in range(4)], axis=0)

    def pieces(p, part):
        start, stop = (0, CUT) if part == A else (CUT, OUT_COLS[p])
        return start, stop - start, [(c, min(256, stop - c)) for c in range(start, stop, 256)]

    swaps = {}

    def give(p, place, part):
        rows = hidden_rows(p, place)
        start, width, cuts = pieces(p, part)
        for c, size in cuts:
            piece = jnp.dot(rows, wd[other, :, pl.ds(OFFSET[p] + c, size)], preferred_element_type=F32)
            xs[p][0, place, :, :, :, pl.ds(c, size)] = piece.astype(BF).reshape(4, 4, ROWS, size)
        swaps[p, place, part] = send(
            xs[p].at[0, place, :, :, :, pl.ds(start, width)], rs[p].at[place, :, :, :, pl.ds(start, width)],
            sum_r.at[p, 2 * place + part], sibling)

    def keep(p, place, part):
        rows = hidden_rows(p, place)
        swaps[p, place, part].wait_recv()
        for c, size in pieces(p, part)[2]:
            piece = jnp.dot(rows, wd[core, :, pl.ds(OFFSET[p] + c, size)], preferred_element_type=F32)
            theirs = rs[p][place, :, :, :, pl.ds(c, size)].reshape(256, size).astype(F32)
            os[p][place, :, :, :, pl.ds(c, size)] = (piece + theirs).astype(BF).reshape(4, 4, ROWS, size)

    def add(ref, *more):
        total = ref[...].astype(F32)
        for one in more:
            total = total + one[...].astype(F32)
        ref[...] = total.astype(BF)

    def sum_view(p, k, place, c, part=None):
        prefix = {0: (0, 0, place), 1: (0, place), 2: (place,)}[k]
        return os[p].at[(*prefix, *cut(chunks_of(k)[c], part, OUT_COLS[p]))]

    def passing_view(p, k, c, part=None):
        return passing[k, p].at[cut(chunks_of(k)[c], part, OUT_COLS[p])]

    def side_view(p, k, n, c, part=None):
        return sides[k, p].at[(n, *cut(chunks_of(k)[c], part, OUT_COLS[p]))]

    def rs_slot(k, c, n):
        return (13, 10, 0)[k] + (2 if k == 2 else 1) * c + n

    def toss(p, k, c, n, src, dst, to):
        send(src, dst, rs_r.at[p, rs_slot(k, c, n)], to[ORDER[p][k]])

    def toss_far_half(p, k, c, part):
        toss(p, k, c, 0, sum_view(p, k, FAR, c, part), passing_view(p, k, c, part), (right, left)[part])

    def toss_far(p, k, c):
        toss_far_half(p, k, c, A)
        toss_far_half(p, k, c, B)

    def toss_right(p, k, c):
        toss(p, k, c, 1, sum_view(p, k, RIGHT, c, B), side_view(p, k, 0, c, B), right)

    def toss_left(p, k, c):
        toss(p, k, c, 1, sum_view(p, k, LEFT, c, A), side_view(p, k, 1, c, A), left)

    def pass_on(p, k, c):
        landed(passing_view(p, k, c), rs_r.at[p, rs_slot(k, c, 0)])
        add(sum_view(p, k, RIGHT, c, A), passing_view(p, k, c, A))
        toss(p, k, c, 1, sum_view(p, k, RIGHT, c, A), side_view(p, k, 0, c, A), right)
        add(sum_view(p, k, LEFT, c, B), passing_view(p, k, c, B))
        toss(p, k, c, 1, sum_view(p, k, LEFT, c, B), side_view(p, k, 1, c, B), left)

    def complete(p, k, c):
        landed(side_view(p, k, slice(None), c), rs_r.at[p, rs_slot(k, c, 1)])
        add(sum_view(p, k, OWN, c), side_view(p, k, 0, c), side_view(p, k, 1, c))

    def straight(p, k):
        for n, place, to in ((0, RIGHT, right), (1, LEFT, left), (2, FAR, far)):
            toss(p, k, 0, 0, sum_view(p, k, place, 0), threes[k, p].at[n], to)

    def straight_done(p, k):
        landed(threes[k, p], rs_r.at[p, rs_slot(k, 0, 0)])
        return [threes[k, p][n] for n in range(3)]

    actions = {
        (FAR, A): lambda p, k, c: toss_far_half(p, k, c, A),
        (FAR, B): lambda p, k, c: toss_far_half(p, k, c, B),
        (RIGHT, B): toss_right,
        (LEFT, A): toss_left,
    }

    def produce(tasks, following):
        for n, task in enumerate(tasks):
            ahead = (tasks + following)[n + LEAD:n + LEAD + 1]
            if ahead:
                give(*ahead[0])
            keep(*task)
            action = actions.get(task[1:])
            if action:
                for c in (4, 3, 1, 2, 0):
                    action(task[0], 2, c)

    tasks = [(p, *half) for half in ((FAR, A), (FAR, B), (RIGHT, B), (LEFT, A), (RIGHT, A), (LEFT, B)) for p in PARTS]
    own_tasks = [(p, OWN, part) for part in (A, B) for p in PARTS]
    for n in range(LEAD):
        give(*tasks[n])
    produce(tasks, own_tasks[:LEAD])
    for p in PARTS:
        pass_on(p, 2, 4)
    for p in PARTS:
        pass_on(p, 2, 3)
    produce(own_tasks, [])
    for p in PARTS:
        pass_on(p, 2, 1)
    for p in PARTS:
        complete(p, 2, 4)
        toss_far(p, 1, 1)
    for p in PARTS:
        pass_on(p, 2, 2)
        pass_on(p, 2, 0)
    for p in PARTS:
        complete(p, 2, 3)
        toss_right(p, 1, 1)
        toss_left(p, 1, 1)
    for p in PARTS:
        complete(p, 2, 1)
        pass_on(p, 1, 1)
    for p in PARTS:
        complete(p, 2, 2)
        straight(p, 1)
    for p in PARTS:
        complete(p, 1, 1)
        straight(p, 0)
    for p in PARTS:
        complete(p, 2, 0)
    here = []
    for p in PARTS:
        total = os[p][0, 0, 0].astype(F32)
        for one in straight_done(p, 1) + straight_done(p, 0):
            total = total + one.astype(F32)
        low, up = total[0:8], total[8:16]
        here.append(jnp.where(core == 0, low, up))
        fin_out[:, pl.ds(OFFSET[p], OUT_COLS[p])] = jnp.where(core == 0, up, low)
    last = send(fin_out, fin_in, end_r.at[1], sibling)
    for p in PARTS:
        at = pl.ds(pl.multiple_of(core * HALF + OFFSET[p], 128), OUT_COLS[p])
        out[:, at] = (tokens[:, at].astype(F32) + here[p]).astype(BF)
    last.wait_recv()
    at = pl.ds(pl.multiple_of(other * HALF, 128), HALF)
    out[:, at] = (tokens[:, at].astype(F32) + fin_in[...]).astype(BF)
    settle()
    pltpu.make_async_copy(packed.at[pl.ds(0, 31)], dbuf.at[pl.ds(0, 31)], d_s).wait()


def fused(tokens, routes, weights, dense_gate, dense_up, dense_down, expert_gate, expert_up, expert_down):
    vmem = pl.BlockSpec(memory_space=pltpu.VMEM)
    hbm = pl.BlockSpec(memory_space=pl.ANY)
    cube = (4, 4, 4, ROWS)
    scratch = [pltpu.VMEM((2, *cube, IN_COLS[p]), BF) for p in PARTS]
    scratch += [pltpu.VMEM((*cube, OUT_COLS[p]), BF) for p in PARTS] * 2
    scratch += [pltpu.VMEM((*(4,) * k, ROWS, OUT_COLS[p]), BF) for k in (1, 2) for p in PARTS]
    scratch += [pltpu.VMEM((2, *(4,) * k, ROWS, OUT_COLS[p]), BF) for k in (1, 2) for p in PARTS]
    scratch += [pltpu.VMEM((3, ROWS, OUT_COLS[p]), BF) for k in (0, 1) for p in PARTS]
    scratch += [
        pltpu.VMEM((3, EXPERT_ROWS, WIDTH), BF),
        pltpu.VMEM((2, UNITS, HALF), BF),
        pltpu.VMEM((2, UNITS, HALF), BF),
        pltpu.VMEM((2, UNITS, HALF), BF),
        pltpu.VMEM((*cube, UNITS), F32),
        pltpu.VMEM((*cube, UNITS), F32),
        pltpu.VMEM((*cube, UNITS), BF),
        pltpu.VMEM((8, HALF + 128), F32),
        pltpu.VMEM((8, HALF + 128), F32),
        pltpu.VMEM((8, HALF), F32),
        pltpu.VMEM((8, HALF), F32),
        pltpu.VMEM((32, 64, 256), BF),
        pltpu.VMEM((32, 64, 256), BF),
        pltpu.SemaphoreType.DMA((3,)),
        pltpu.SemaphoreType.DMA,
        pltpu.SemaphoreType.DMA,
        pltpu.SemaphoreType.DMA((FLIGHTS,)),
        pltpu.SemaphoreType.DMA((3, 15)),
        pltpu.SemaphoreType.DMA((3, 5)),
        pltpu.SemaphoreType.DMA((3, 14)),
        pltpu.SemaphoreType.DMA((3, 8)),
        pltpu.SemaphoreType.DMA((2,)),
    ]
    return pl.pallas_call(
        kernel,
        out_shape=jax.ShapeDtypeStruct((8, WIDTH), BF),
        in_specs=[vmem] * 6 + [hbm] * 3,
        out_specs=vmem,
        scratch_shapes=scratch,
        cost_estimate=pl.CostEstimate(flops=2 * 1024 * 192 * 7168 * 3, bytes_accessed=8_000_000, transcendentals=1024 * 192),
        compiler_params=pltpu.CompilerParams(
            collective_id=0, has_side_effects=True, vmem_limit_bytes=63 * 2**20),
    )(tokens, routes, weights, dense_gate, dense_up, dense_down, expert_gate, expert_up, expert_down)


def per_device(tokens, routes, gate_weights, dense_gate, dense_up, dense_down, expert_gate, expert_up, expert_down):
    return fused(
        tokens, routes.T, gate_weights.T, dense_gate, dense_up, dense_down, expert_gate, expert_up, expert_down)


def solution(mesh):
    return jax.shard_map(
        per_device,
        mesh=mesh,
        in_specs=(
            P(("ep", "tp"), None),
            P(("ep", "tp"), None),
            P(("ep", "tp"), None),
            P("ep", "tp"),
            P("ep", "tp"),
            P("ep", "tp"),
            P("tp", "ep", None),
            P("tp", "ep", None),
            P("tp", "ep", None),
        ),
        out_specs=P(("ep", "tp"), None),
        check_vma=False,
    )
```

```python
import jax
import jax.numpy as jnp
from jax import lax
from jax.experimental import pallas as pl
from jax.experimental.pallas import tpu as pltpu
from jax.sharding import PartitionSpec as P

MESH = pl.DeviceIdType.MESH
BF = jnp.bfloat16
F32 = jnp.float32

WIDTH = 7168
HALF = WIDTH // 2
ROWS = 16
UNITS = 192
DENSE_ROWS = 32
EXPERT_ROWS = 152
DEPTH = 224
RUN = 4 * DEPTH
OUT_COLS = (1280, 1152, 1152)
OFFSET = (0, 1280, 2432)
IN_COLS = (1280, 1152, 1280)
CUT = 640
ORDER = (("y", "x", "z"), ("z", "y", "x"), ("x", "z", "y"))
PARTS = range(3)
OWN, RIGHT, LEFT, FAR = range(4)
BOTH = pl.ds(1, 2)
OTHERS = pl.ds(1, 3)
LINE = (0, OTHERS)
PLANE = ((0, 0), (0, OTHERS), (OTHERS, 0), (BOTH, OTHERS), (3, OTHERS))
A, B = 0, 1
LEAD = 3
FLIGHTS = 48


def cut(selected, part, cols):
    if part is None:
        return tuple(selected)
    side = pl.ds(0, CUT) if part == A else pl.ds(CUT, cols - CUT)
    return (*selected, slice(None), side)


def view(ref, index):
    return ref.at[index] if index else ref


def kernel(
    tokens, routes, weights, dense_gate, dense_up, dense_down, expert_gate, expert_up, expert_down,
    out,
    x0, x1, x2, o0, o1, o2, r0, r1, r2,
    *rest,
):
    xs, os, rs = (x0, x1, x2), (o0, o1, o2), (r0, r1, r2)
    passing = {(k, p): rest[(k - 1) * 3 + p] for k in (1, 2) for p in PARTS}
    sides = {(k, p): rest[6 + (k - 1) * 3 + p] for k in (1, 2) for p in PARTS}
    threes = {(k, p): rest[12 + k * 3 + p] for k in (0, 1) for p in PARTS}
    rest = rest[18:]
    (raw, wg, wu, wd, ga, ua, hid, tok_out, tok_in, fin_out, fin_in, packed, dbuf,
     w_sem, d_s, d_r, out_s, ag_r, sib_r, rs_r, sum_r, end_r) = rest

    ep, tp = lax.axis_index("ep"), lax.axis_index("tp")
    core = lax.rem(tp, 2)
    other = 1 - core
    pos = {
        "x": lax.div(ep, 8),
        "y": lax.div(tp, 2) * 2 + lax.rem(lax.div(ep, 4), 2),
        "z": lax.rem(ep, 4),
    }

    def device(x, y, z):
        return {"ep": x * 8 + lax.rem(y, 2) * 4 + z, "tp": lax.div(y, 2) * 2 + core}

    def moved(axis, by):
        place = dict(pos)
        place[axis] = lax.rem(pos[axis] + by, 4)
        return device(place["x"], place["y"], place["z"])

    right = {a: moved(a, 1) for a in "xyz"}
    left = {a: moved(a, 3) for a in "xyz"}
    far = {a: moved(a, 2) for a in "xyz"}
    sibling = {"ep": ep, "tp": lax.div(tp, 2) * 2 + other}

    loads = [
        pltpu.make_async_copy(w.at[0], raw.at[n], w_sem.at[n])
        for n, w in enumerate((expert_gate, expert_up, expert_down))
    ]
    for load in loads:
        load.start()

    y_low = lax.rem(pos["y"], 2)
    steps = sorted(
        ((dx, dy, dz) for dx in range(4) for dy in range(2) for dz in range(4) if dx or dy or dz),
        key=lambda d: min(d[0], 4 - d[0]) + d[1] + min(d[2], 4 - d[2]))

    def peer(dx, dy, dz):
        return lax.rem(pos["x"] + dx, 4) * 8 + lax.rem(y_low + dy, 2) * 4 + lax.rem(pos["z"] + dz, 4)

    peers = [peer(*d) for d in steps]

    barrier = pltpu.get_barrier_semaphore()
    pl.semaphore_signal(barrier, inc=1, device_id=sibling, device_id_type=MESH)
    for by in (1, 2, 3):
        pl.semaphore_signal(barrier, inc=1, device_id=moved("y", by), device_id_type=MESH)
    for d, to in zip(steps, peers):
        if d != (0, 1, 0):
            pl.semaphore_signal(barrier, inc=1, device_id={"ep": to, "tp": tp}, device_id_type=MESH)
    pl.semaphore_wait(barrier, 34)

    flying = []

    def send(src, dst, r_sem, to):
        n = len(flying)
        if n >= FLIGHTS:
            flying[n - FLIGHTS].wait_send()
        copy = pltpu.make_async_remote_copy(
            src_ref=src, dst_ref=dst, send_sem=out_s.at[n % FLIGHTS], recv_sem=r_sem, device_id=to, device_id_type=MESH)
        copy.start()
        flying.append(copy)
        return copy

    def settle():
        for copy in flying[max(0, len(flying) - FLIGHTS):]:
            copy.wait_send()
        flying.clear()

    def landed(ref, sem):
        pltpu.make_async_copy(ref, ref, sem).wait()

    diagonal = lax.broadcasted_iota(jnp.int32, (8, 8), 0) == lax.broadcasted_iota(jnp.int32, (8, 8), 1)

    def column_of(row):
        return jnp.sum(jnp.where(diagonal, jnp.broadcast_to(row, (8, 8)), jnp.zeros((8, 8), row.dtype)), axis=1, keepdims=True)

    lane = lax.broadcasted_iota(jnp.int32, (8, 128), 1)
    named = lax.div(lane, 2).astype(F32)
    chosen = [column_of(routes[n:n + 1, :].astype(F32)) for n in range(2)]
    factor = jnp.where(chosen[0] == named, column_of(weights[0:1, :]), 0.0) + jnp.where(
        chosen[1] == named, column_of(weights[1:2, :]), 0.0)
    high = factor.astype(BF).astype(F32)
    factor = jnp.where(lax.rem(lane, 2) == 0, high, factor - high)
    tok_out[:, pl.ds(0, HALF)] = tokens[:, pl.ds(pl.multiple_of(other * HALF, 128), HALF)].astype(F32)
    tok_out[:, pl.ds(HALF, 128)] = factor
    swap = send(tok_out, tok_in, end_r.at[0], sibling)
    swap.wait_recv()
    for p in PARTS:
        mine = tokens[:, pl.ds(pl.multiple_of(core * HALF + OFFSET[p], 128), OUT_COLS[p])].astype(F32)
        if IN_COLS[p] > OUT_COLS[p]:
            mine = jnp.concatenate([mine, factor], axis=1)
        theirs = tok_in[:, pl.ds(OFFSET[p], IN_COLS[p])]
        first = jnp.where(core == 0, mine, theirs)
        second = jnp.where(core == 0, theirs, mine)
        xs[p][core, 0, 0, 0] = jnp.concatenate([first, second], axis=0).astype(BF)

    def chunks_of(k):
        return ((),) if k == 0 else tuple((s,) for s in LINE) if k == 1 else PLANE

    def token_view(p, k, place, c, part=None):
        prefix = {0: (core, 0, 0, place), 1: (core, 0, place), 2: (core, place)}[k]
        return xs[p].at[(*prefix, *cut(chunks_of(k)[c], part, IN_COLS[p]))]

    def ag_slot(k, c, n):
        return 0 if k == 0 else (0, 1, 5)[k] + 2 * c + n

    def fly(p, k, c, n, src, dst, to):
        send(src, dst, ag_r.at[p, ag_slot(k, c, n)], to[ORDER[p][k]])

    def spread(p, k, c=0, direct=False):
        own = token_view(p, k, OWN, c)
        fly(p, k, c, 0, own, token_view(p, k, LEFT, c), right)
        fly(p, k, c, 0, own, token_view(p, k, RIGHT, c), left)
        if direct:
            fly(p, k, c, 1, own, token_view(p, k, FAR, c), far)

    def near(p, k, c=0):
        landed(token_view(p, k, OTHERS if k == 0 else BOTH, c), ag_r.at[p, ag_slot(k, c, 0)])

    def relay(p, k, c=0):
        near(p, k, c)
        fly(p, k, c, 1, token_view(p, k, LEFT, c, A), token_view(p, k, FAR, c, A), right)
        fly(p, k, c, 1, token_view(p, k, RIGHT, c, B), token_view(p, k, FAR, c, B), left)

    def distant(p, k, c=0):
        landed(token_view(p, k, FAR, c), ag_r.at[p, ag_slot(k, c, 1)])

    shares = {}

    def share(p, n, ref):
        shares[p, n] = send(ref, ref, sib_r.at[p, n], sibling)

    def where(p, third, second, first):
        place = dict(zip(ORDER[p], (first, second, third)))
        return place["y"], place["z"], place["x"]

    def gate_up(p, place, h):
        cols = OUT_COLS[p]
        rows = xs[p][h, place, :, :, :, pl.ds(0, cols)].reshape(256, cols)
        for w, acc in ((wg, ga), (wu, ua)):
            piece = lax.dot_general(
                rows, w[h, :, pl.ds(OFFSET[p], cols)], (((1,), (1,)), ((), ())), preferred_element_type=F32)
            for i in range(4):
                for j in range(4):
                    n = (i * 4 + j) * ROWS
                    acc[where(p, place, i, j)] += piece[n:n + ROWS]

    def dense_pack():
        tails, later = [], []
        for n, w in enumerate((dense_gate, dense_up, dense_down)):
            rows = jnp.concatenate([w[...].astype(F32), jnp.zeros((256 - DEPTH, 640), F32)], axis=0)
            turned = rows.T
            packed[:, pl.ds(16 * n, 16), :] = turned[:512, :128].astype(BF).reshape(32, 16, 128)
            later.append(turned[:512, 128:])
            tails.append(turned[512:].astype(BF))
        place = lax.broadcasted_iota(jnp.int32, (512, 384), 0)
        unit = lax.broadcasted_iota(jnp.int32, (512, 384), 1)
        to, row = lax.div(place, 16), lax.rem(place, 16)
        wanted = lax.div(row, 4) * 128 + to * 4 + lax.rem(row, 4)
        pick = jnp.where(unit == wanted, 1.0, 0.0).astype(BF)
        moved_rows = jnp.dot(pick, jnp.concatenate(tails, axis=0), preferred_element_type=F32)
        packed[:, pl.ds(48, 16), :] = moved_rows[:, :128].astype(BF).reshape(32, 16, 128)
        spare = lax.broadcasted_iota(jnp.int32, (512, 128), 1) >= 96
        for n in range(3):
            ridden = pltpu.roll(moved_rows[:, 128:], 96 - 32 * n, 1)
            both = jnp.where(spare, ridden, later[n])
            packed[:, pl.ds(64 + 16 * n, 16), :] = both.astype(BF).reshape(32, 16, 128)
        pltpu.make_async_copy(packed.at[ep], dbuf.at[ep], d_r).start()

    def dense_out(first, last):
        for to in peers[first:last]:
            pltpu.make_async_remote_copy(
                src_ref=packed.at[to], dst_ref=dbuf.at[ep], send_sem=d_s, recv_sem=d_r,
                device_id={"ep": to, "tp": tp}, device_id_type=MESH).start()

    def unpacked(source):
        block = dbuf[source].astype(F32)
        lanes = lax.div(lax.broadcasted_iota(jnp.int32, (16, 128), 1), 32)
        tail = jnp.zeros((16, 128), F32)
        for n in range(3):
            ridden = pltpu.roll(block[64 + 16 * n:80 + 16 * n], (32 + 32 * n) % 128, 1)
            tail = jnp.where(lanes == n, ridden, tail)
        return jnp.concatenate([block[0:64], jnp.concatenate([block[64:112], tail], axis=0)], axis=1)

    def dense_in():
        landed(dbuf, d_r)
        row = lax.broadcasted_iota(jnp.int32, (ROWS, RUN), 0)
        for i in range(8):
            at = pl.ds((i % 4) * RUN, RUN)
            run = jnp.concatenate([unpacked(4 * i + z)[:, 0:DEPTH] for z in range(4)], axis=1)
            tail = run[48:64]
            for n, w in enumerate((wg, wu, wd)):
                w[i // 4, pl.ds(0, 16), at] = run[16 * n:16 * n + 16].astype(BF)
                turned = tail if n == 0 else pltpu.roll(tail, 16 - 4 * n, 0)
                w[i // 4, pl.ds(16, 16), at] = jnp.where(row < 4, turned, 0.0).astype(BF)

    def expert_in():
        for load in loads[:3]:
            load.wait()
        for n, w in enumerate((wg, wu, wd)):
            for h in range(2):
                w[h, pl.ds(176, 16)] = jnp.zeros((16, HALF), BF)
                w[h, pl.ds(DENSE_ROWS, EXPERT_ROWS)] = raw[n, :, pl.ds(h * HALF, HALF)]
        ga[...] = jnp.zeros_like(ga)
        ua[...] = jnp.zeros_like(ua)

    for p in PARTS:
        spread(p, 0, direct=True)
    for p in PARTS:
        spread(p, 1, 0, direct=True)
    for p in PARTS:
        spread(p, 2, 0)
    dense_pack()
    dense_out(0, 16)
    for p in PARTS:
        near(p, 0)
        spread(p, 1, 1, direct=True)
        spread(p, 2, 1)
    dense_out(16, 24)
    for p in PARTS:
        near(p, 1, 0)
        distant(p, 1, 0)
        spread(p, 2, 2)
    dense_out(24, 31)
    for p in PARTS:
        relay(p, 2, 0)
    for p in PARTS:
        near(p, 1, 1)
        spread(p, 2, 3)
    for p in PARTS:
        distant(p, 1, 1)
        spread(p, 2, 4)
        share(p, 0, xs[p].at[core, 0])
    expert_in()
    for p in PARTS:
        relay(p, 2, 1)
    for p in PARTS:
        relay(p, 2, 2)
    dense_in()
    for p in PARTS:
        relay(p, 2, 3)
    for p in PARTS:
        gate_up(p, OWN, core)
    for p in PARTS:
        relay(p, 2, 4)
        share(p, 1, xs[p].at[core, RIGHT])
        share(p, 2, xs[p].at[core, LEFT])
    for p in PARTS:
        shares[p, 0].wait_recv()
        gate_up(p, OWN, other)
    for p in PARTS:
        gate_up(p, RIGHT, core)
        gate_up(p, LEFT, core)
    for p in PARTS:
        for c in (0, 1):
            distant(p, 2, c)
        share(p, 3, xs[p].at[core, FAR, 0])
    for p in PARTS:
        shares[p, 1].wait_recv()
        gate_up(p, RIGHT, other)
        shares[p, 2].wait_recv()
        gate_up(p, LEFT, other)
    for p in PARTS:
        for c in (2, 3, 4):
            distant(p, 2, c)
        share(p, 4, xs[p].at[core, FAR, OTHERS])
    for p in PARTS:
        gate_up(p, FAR, core)
    for p in PARTS:
        shares[p, 3].wait_recv()
        shares[p, 4].wait_recv()
        gate_up(p, FAR, other)

    lanes = lax.broadcasted_iota(jnp.int32, (256, 128), 1)
    column = lax.broadcasted_iota(jnp.int32, (256, UNITS), 1)
    for y in range(4):
        sent = x2[0, y, :, :, :, pl.ds(OUT_COLS[2], 128)].reshape(256, 128).astype(F32)
        share_of = jnp.sum(jnp.where(lax.div(lanes, 2) == tp, sent, 0.0), axis=1, keepdims=True)
        g = ga[y].reshape(256, UNITS)
        u = ua[y].reshape(256, UNITS)
        value = g / (1.0 + jnp.exp(-g)) * u
        value = value * jnp.where(column < DENSE_ROWS, 1.0, share_of)
        hid[y] = value.astype(BF).reshape(4, 4, ROWS, UNITS)

    settle()

    def hidden_rows(p, place):
        return jnp.concatenate([hid[where(p, place, i, j)] for i in range(4) for j in range(4)], axis=0)

    def pieces(p, part):
        start, stop = (0, CUT) if part == A else (CUT, OUT_COLS[p])
        return start, stop - start, [(c, min(256, stop - c)) for c in range(start, stop, 256)]

    swaps = {}

    def give(p, place, part):
        rows = hidden_rows(p, place)
        start, width, cuts = pieces(p, part)
        for c, size in cuts:
            piece = jnp.dot(rows, wd[other, :, pl.ds(OFFSET[p] + c, size)], preferred_element_type=F32)
            xs[p][0, place, :, :, :, pl.ds(c, size)] = piece.astype(BF).reshape(4, 4, ROWS, size)
        swaps[p, place, part] = send(
            xs[p].at[0, place, :, :, :, pl.ds(start, width)], rs[p].at[place, :, :, :, pl.ds(start, width)],
            sum_r.at[p, 2 * place + part], sibling)

    def keep(p, place, part):
        rows = hidden_rows(p, place)
        swaps[p, place, part].wait_recv()
        for c, size in pieces(p, part)[2]:
            piece = jnp.dot(rows, wd[core, :, pl.ds(OFFSET[p] + c, size)], preferred_element_type=F32)
            theirs = rs[p][place, :, :, :, pl.ds(c, size)].reshape(256, size).astype(F32)
            os[p][place, :, :, :, pl.ds(c, size)] = (piece + theirs).astype(BF).reshape(4, 4, ROWS, size)

    def add(ref, *more):
        total = ref[...].astype(F32)
        for one in more:
            total = total + one[...].astype(F32)
        ref[...] = total.astype(BF)

    def sum_view(p, k, place, c, part=None):
        prefix = {0: (0, 0, place), 1: (0, place), 2: (place,)}[k]
        return os[p].at[(*prefix, *cut(chunks_of(k)[c], part, OUT_COLS[p]))]

    def passing_view(p, k, c, part=None):
        return passing[k, p].at[cut(chunks_of(k)[c], part, OUT_COLS[p])]

    def side_view(p, k, n, c, part=None):
        return sides[k, p].at[(n, *cut(chunks_of(k)[c], part, OUT_COLS[p]))]

    def rs_slot(k, c, n):
        return (13, 10, 0)[k] + (2 if k == 2 else 1) * c + n

    def toss(p, k, c, n, src, dst, to):
        send(src, dst, rs_r.at[p, rs_slot(k, c, n)], to[ORDER[p][k]])

    def toss_far_half(p, k, c, part):
        toss(p, k, c, 0, sum_view(p, k, FAR, c, part), passing_view(p, k, c, part), (right, left)[part])

    def toss_far(p, k, c):
        toss_far_half(p, k, c, A)
        toss_far_half(p, k, c, B)

    def toss_right(p, k, c):
        toss(p, k, c, 1, sum_view(p, k, RIGHT, c, B), side_view(p, k, 0, c, B), right)

    def toss_left(p, k, c):
        toss(p, k, c, 1, sum_view(p, k, LEFT, c, A), side_view(p, k, 1, c, A), left)

    def pass_on(p, k, c):
        landed(passing_view(p, k, c), rs_r.at[p, rs_slot(k, c, 0)])
        add(sum_view(p, k, RIGHT, c, A), passing_view(p, k, c, A))
        toss(p, k, c, 1, sum_view(p, k, RIGHT, c, A), side_view(p, k, 0, c, A), right)
        add(sum_view(p, k, LEFT, c, B), passing_view(p, k, c, B))
        toss(p, k, c, 1, sum_view(p, k, LEFT, c, B), side_view(p, k, 1, c, B), left)

    def complete(p, k, c):
        landed(side_view(p, k, slice(None), c), rs_r.at[p, rs_slot(k, c, 1)])
        add(sum_view(p, k, OWN, c), side_view(p, k, 0, c), side_view(p, k, 1, c))

    def straight(p, k):
        for n, place, to in ((0, RIGHT, right), (1, LEFT, left), (2, FAR, far)):
            toss(p, k, 0, 0, sum_view(p, k, place, 0), threes[k, p].at[n], to)

    def straight_done(p, k):
        landed(threes[k, p], rs_r.at[p, rs_slot(k, 0, 0)])
        return [threes[k, p][n] for n in range(3)]

    actions = {
        (FAR, A): lambda p, k, c: toss_far_half(p, k, c, A),
        (FAR, B): lambda p, k, c: toss_far_half(p, k, c, B),
        (RIGHT, B): toss_right,
        (LEFT, A): toss_left,
    }

    def produce(tasks, following):
        for n, task in enumerate(tasks):
            ahead = (tasks + following)[n + LEAD:n + LEAD + 1]
            if ahead:
                give(*ahead[0])
            keep(*task)
            action = actions.get(task[1:])
            if action:
                for c in (4, 3, 1, 2, 0):
                    action(task[0], 2, c)

    tasks = [(p, *half) for half in ((FAR, A), (FAR, B), (RIGHT, B), (LEFT, A), (RIGHT, A), (LEFT, B)) for p in PARTS]
    own_tasks = [(p, OWN, part) for part in (A, B) for p in PARTS]
    for n in range(LEAD):
        give(*tasks[n])
    produce(tasks, own_tasks[:LEAD])
    for p in PARTS:
        pass_on(p, 2, 4)
    for p in PARTS:
        pass_on(p, 2, 3)
    produce(own_tasks, [])
    for p in PARTS:
        pass_on(p, 2, 1)
    for p in PARTS:
        complete(p, 2, 4)
        toss_far(p, 1, 1)
    for p in PARTS:
        pass_on(p, 2, 2)
        pass_on(p, 2, 0)
    for p in PARTS:
        complete(p, 2, 3)
        toss_right(p, 1, 1)
        toss_left(p, 1, 1)
    for p in PARTS:
        complete(p, 2, 1)
        pass_on(p, 1, 1)
    for p in PARTS:
        complete(p, 2, 2)
        straight(p, 1)
    for p in PARTS:
        complete(p, 1, 1)
        straight(p, 0)
    for p in PARTS:
        complete(p, 2, 0)
    here = []
    for p in PARTS:
        total = os[p][0, 0, 0].astype(F32)
        for one in straight_done(p, 1) + straight_done(p, 0):
            total = total + one.astype(F32)
        low, up = total[0:8], total[8:16]
        here.append(jnp.where(core == 0, low, up))
        fin_out[:, pl.ds(OFFSET[p], OUT_COLS[p])] = jnp.where(core == 0, up, low)
    last = send(fin_out, fin_in, end_r.at[1], sibling)
    for p in PARTS:
        at = pl.ds(pl.multiple_of(core * HALF + OFFSET[p], 128), OUT_COLS[p])
        out[:, at] = (tokens[:, at].astype(F32) + here[p]).astype(BF)
    last.wait_recv()
    at = pl.ds(pl.multiple_of(other * HALF, 128), HALF)
    out[:, at] = (tokens[:, at].astype(F32) + fin_in[...]).astype(BF)
    settle()
    pltpu.make_async_copy(packed.at[pl.ds(0, 31)], dbuf.at[pl.ds(0, 31)], d_s).wait()


def fused(tokens, routes, weights, dense_gate, dense_up, dense_down, expert_gate, expert_up, expert_down):
    vmem = pl.BlockSpec(memory_space=pltpu.VMEM)
    hbm = pl.BlockSpec(memory_space=pl.ANY)
    cube = (4, 4, 4, ROWS)
    scratch = [pltpu.VMEM((2, *cube, IN_COLS[p]), BF) for p in PARTS]
    scratch += [pltpu.VMEM((*cube, OUT_COLS[p]), BF) for p in PARTS] * 2
    scratch += [pltpu.VMEM((*(4,) * k, ROWS, OUT_COLS[p]), BF) for k in (1, 2) for p in PARTS]
    scratch += [pltpu.VMEM((2, *(4,) * k, ROWS, OUT_COLS[p]), BF) for k in (1, 2) for p in PARTS]
    scratch += [pltpu.VMEM((3, ROWS, OUT_COLS[p]), BF) for k in (0, 1) for p in PARTS]
    scratch += [
        pltpu.VMEM((3, EXPERT_ROWS, WIDTH), BF),
        pltpu.VMEM((2, UNITS, HALF), BF),
        pltpu.VMEM((2, UNITS, HALF), BF),
        pltpu.VMEM((2, UNITS, HALF), BF),
        pltpu.VMEM((*cube, UNITS), F32),
        pltpu.VMEM((*cube, UNITS), F32),
        pltpu.VMEM((*cube, UNITS), BF),
        pltpu.VMEM((8, HALF + 128), F32),
        pltpu.VMEM((8, HALF + 128), F32),
        pltpu.VMEM((8, HALF), F32),
        pltpu.VMEM((8, HALF), F32),
        pltpu.VMEM((32, 112, 128), BF),
        pltpu.VMEM((32, 112, 128), BF),
        pltpu.SemaphoreType.DMA((3,)),
        pltpu.SemaphoreType.DMA,
        pltpu.SemaphoreType.DMA,
        pltpu.SemaphoreType.DMA((FLIGHTS,)),
        pltpu.SemaphoreType.DMA((3, 15)),
        pltpu.SemaphoreType.DMA((3, 5)),
        pltpu.SemaphoreType.DMA((3, 14)),
        pltpu.SemaphoreType.DMA((3, 8)),
        pltpu.SemaphoreType.DMA((2,)),
    ]
    return pl.pallas_call(
        kernel,
        out_shape=jax.ShapeDtypeStruct((8, WIDTH), BF),
        in_specs=[vmem] * 6 + [hbm] * 3,
        out_specs=vmem,
        scratch_shapes=scratch,
        cost_estimate=pl.CostEstimate(flops=2 * 1024 * 192 * 7168 * 3, bytes_accessed=8_000_000, transcendentals=1024 * 192),
        compiler_params=pltpu.CompilerParams(
            collective_id=0, has_side_effects=True, vmem_limit_bytes=63 * 2**20),
    )(tokens, routes, weights, dense_gate, dense_up, dense_down, expert_gate, expert_up, expert_down)


def per_device(tokens, routes, gate_weights, dense_gate, dense_up, dense_down, expert_gate, expert_up, expert_down):
    return fused(
        tokens, routes.T, gate_weights.T, dense_gate, dense_up, dense_down, expert_gate, expert_up, expert_down)


def solution(mesh):
    return jax.shard_map(
        per_device,
        mesh=mesh,
        in_specs=(
            P(("ep", "tp"), None),
            P(("ep", "tp"), None),
            P(("ep", "tp"), None),
            P("ep", "tp"),
            P("ep", "tp"),
            P("ep", "tp"),
            P("tp", "ep", None),
            P("tp", "ep", None),
            P("tp", "ep", None),
        ),
        out_specs=P(("ep", "tp"), None),
        check_vma=False,
    )
```
